128 devices in a mesh: space: 16 (over y, z), chan: 8 (over x, core).
Axes of the slice: x: 4, y: 4, z: 4, core: 2. Of those that a mesh axis runs over, the one named last changes fastest.
Arguments:
- field: float32 [128, 512, 512], P('chan', 'space'), may hold values from -6 to 6
- gain_one: float32 [128], P('chan'), may hold values from 0.1 to 1.9
- spec_one: float32 [2, 16, 8, 8], P(None, 'chan'), may hold values from -1.5 to 1.5
- spec_two: float32 [2, 16, 8, 8], P(None, 'chan'), may hold values from -2 to 2
- gain_two: float32 [128], replicated, may hold values from 0.1 to 1.9
- mlp_in: float32 [512, 128], replicated, may hold values from -0.5 to 0.5
- mlp_out: float32 [128, 512], replicated, may hold values from -0.25 to 0.25
Outputs:
- result: float32 [128, 512, 512], P('chan', 'space')
The draws below stay inside these ranges and needn't reach their ends.
All inputs are finite; a program needn't handle non-finite values.
Results may differ from the reference program's by a relative error of at most 0.00011.
Values sent between devices are 32-bit elements; how exact they have to be, the bound alone decides.
A program may use at most 128 MiB of HBM per device.

```python
import jax
import jax.numpy as jnp
from jax import lax

H = 512
W = 512
C = 128
HID = 512
NB = 16
BS = 8


def block_scale(stream_key, shape, split, low, high):
    def one(position, shards_of):
        heights = jax.random.uniform(jax.random.fold_in(jax.random.fold_in(stream_key, 6), position), (shards_of,), jnp.float32, low / len(split), high / len(split))
        return jnp.repeat(jnp.exp(heights), shape[position] // shards_of).reshape((-1,) + (1,) * (len(shape) - position - 1))

    level = one(*split[0])
    for cut in split[1:]:
        level = level * one(*cut)
    return level


def normal_values(own_key, extent, scale, limit, cuts=(), held_as=jnp.bfloat16):
    factor_of = block_scale(own_key, extent, cuts, -0.22, 0.18) if cuts else 1.0
    result = jax.random.normal(own_key, extent, jnp.float32) * scale * factor_of
    return jnp.minimum(jnp.maximum(result, -limit), limit).astype(held_as)


def setup_inputs(seed: int = 0) -> dict:
    key_list = jax.random.split(jax.random.key(seed), 8)
    field = normal_values(key_list[0], (C, H, W), 1.0, 6.0, ((0, 8), (1, 16)), jnp.float32)
    gain_one = jnp.clip(1.0 + 0.18 * jax.random.normal(key_list[1], (C,), jnp.float32), 0.1, 1.9)
    spec_one = normal_values(key_list[2], (2, NB, BS, BS), (2 * BS) ** -0.5, 1.5, ((1, 8),), jnp.float32)
    spec_two = normal_values(key_list[3], (2, NB, BS, BS), BS ** -0.5, 2.0, ((1, 8),), jnp.float32)
    gain_two = jnp.clip(1.0 + 0.18 * jax.random.normal(key_list[4], (C,), jnp.float32), 0.1, 1.9)
    mlp_in = normal_values(key_list[5], (HID, C), C ** -0.5, 0.5, (), jnp.float32)
    mlp_out = normal_values(key_list[6], (C, HID), HID ** -0.5, 0.25, (), jnp.float32)
    return {"field": field, "gain_one": gain_one, "spec_one": spec_one, "spec_two": spec_two, "gain_two": gain_two, "mlp_in": mlp_in, "mlp_out": mlp_out}


def layer_norm(values, gain):
    mean = lax.optimization_barrier(jnp.mean(values, axis=0))
    spread = lax.optimization_barrier(jnp.mean((values - mean) ** 2, axis=0))
    return (values - mean) * lax.rsqrt(spread + 1e-05) * gain[:, None, None]

def block_product(real_part, imag_part, weights):
    hi = lax.Precision.HIGHEST
    out_real = jnp.einsum('nihw,nio->nohw', real_part, weights[0], precision=hi) - jnp.einsum('nihw,nio->nohw', imag_part, weights[1], precision=hi)
    out_imag = jnp.einsum('nihw,nio->nohw', imag_part, weights[0], precision=hi) + jnp.einsum('nihw,nio->nohw', real_part, weights[1], precision=hi)
    return (out_real, out_imag)

def shrink(values):
    return jnp.maximum(values - 0.01, 0.0) + jnp.minimum(values + 0.01, 0.0)

def reference(field, gain_one, spec_one, spec_two, gain_two, mlp_in, mlp_out):
    normed = layer_norm(field, gain_one)
    spectrum = jnp.fft.fft2(normed, axes=(1, 2), norm='ortho')
    real_part = jnp.real(spectrum).reshape(NB, BS, H, W)
    imag_part = jnp.imag(spectrum).reshape(NB, BS, H, W)
    first_real, first_imag = block_product(real_part, imag_part, spec_one)
    first_real = jnp.maximum(first_real, 0.0)
    first_imag = jnp.maximum(first_imag, 0.0)
    second_real, second_imag = block_product(first_real, first_imag, spec_two)
    second = (shrink(second_real) + 1j * shrink(second_imag)).reshape(C, H, W)
    mixed = field + jnp.real(jnp.fft.ifft2(second, axes=(1, 2), norm='ortho'))
    normed_two = layer_norm(mixed, gain_two)
    hidden = jax.nn.gelu(jnp.einsum('dc,chw->dhw', mlp_in, normed_two, precision=lax.Precision.HIGHEST), approximate=False)
    return mixed + jnp.einsum('cd,dhw->chw', mlp_out, hidden, precision=lax.Precision.HIGHEST)
```

```python
import functools

import jax
import jax.numpy as jnp
import ml_dtypes
import numpy as np
from jax import lax
from jax.experimental import pallas as pl
from jax.experimental.pallas import tpu as pltpu
from jax.sharding import PartitionSpec as P

MESH = pl.DeviceIdType.MESH
F32 = jnp.float32
BF16 = jnp.bfloat16

H = 512
C = 128
HID = 512
NS = 16
NC = 8
CL = C // NC
HL = H // NS
BS = 8
NBL = CL // BS
KC = 16
ROWS = BS * 2 * KC
LANES = BS * HL

NN = ((1,), (0,))
NT = ((1,), (1,))


def halves(table):
    high = table.astype(ml_dtypes.bfloat16)
    low = (table - high.astype(np.float64)).astype(ml_dtypes.bfloat16)
    return np.stack([high, low])


def width_table():
    row = np.arange(H)
    freq = (row // 32) * KC + row % KC
    imag = (row // KC) % 2 == 1
    nyquist = imag & (freq == 0)
    freq = np.where(nyquist, H // 2, freq)
    angle = 2 * np.pi / H * (freq[:, None] * np.arange(H)[None, :] % H)
    table = np.where((imag & ~nyquist)[:, None], -np.sin(angle), np.cos(angle)) / np.sqrt(H)
    return halves(table)


def height_table():
    series = np.arange(H)
    angle = 2 * np.pi / H * (series[:, None] * series[None, :] % H)
    return halves(np.concatenate([np.cos(angle), np.sin(angle)], axis=1) / np.sqrt(H))


def block_signs():
    row = np.arange(2 * ROWS)[:, None]
    col = np.arange(ROWS)[None, :]
    variant, part_out, part_in = row // ROWS, row // KC % 2, col // KC % 2
    same = row % KC == col % KC
    real = np.where(part_out == part_in, np.where((variant == 1) & (part_out == 1), -1.0, 1.0), 0.0)
    imag = np.where(part_out != part_in, np.where((variant == 0) & (part_out == 0), -1.0, 1.0), 0.0)
    return np.stack([real * same, imag * same]).astype(np.float32)


def channel_lift():
    row = np.arange(2 * ROWS)
    return (row[:, None] // (2 * KC) % BS == np.arange(BS)[None, :]).astype(np.float32)


def split(x):
    high = x.astype(BF16)
    return high, (x - high.astype(F32)).astype(BF16)


def dot(a, b, dims=NN):
    return lax.dot_general(a, b, (dims, ((), ())), preferred_element_type=F32)


def dot3(a, b, dims=NN):
    return dot(a[0], b[0], dims) + (dot(a[0], b[1], dims) + dot(a[1], b[0], dims))


def exact_dot(a, b, dims=NN):
    return lax.dot_general(a, b, (dims, ((), ())), precision=lax.Precision.HIGHEST, preferred_element_type=F32)


def shrink(v):
    return jnp.maximum(v - 0.01, 0.0) + jnp.minimum(v + 0.01, 0.0)


def swap_quarters(t):
    lane = lax.broadcasted_iota(jnp.int32, t[0].shape, 1)
    low = lane < 64
    even = lane % 64 < 32
    u0 = jnp.where(low, t[0], pltpu.roll(t[2], 64, 1))
    u2 = jnp.where(low, pltpu.roll(t[0], 64, 1), t[2])
    u1 = jnp.where(low, t[1], pltpu.roll(t[3], 64, 1))
    u3 = jnp.where(low, pltpu.roll(t[1], 64, 1), t[3])
    v0 = jnp.where(even, u0, pltpu.roll(u1, 32, 1))
    v1 = jnp.where(even, pltpu.roll(u0, 96, 1), u1)
    v2 = jnp.where(even, u2, pltpu.roll(u3, 32, 1))
    v3 = jnp.where(even, pltpu.roll(u2, 96, 1), u3)
    return v0, v1, v2, v3


def kernel(
    gain_one, spec_one, spec_two, gain_two, field, mlp_in, mlp_out, width, height, signs, lift, out,
    f, wd, ht, sg, lf, w1f, w2f, w1h, w1l, w2h, w2l, m1h, m1l, m2h, m2l, x1h, x1l, x2h, x2l,
    part, parts, moments, nh, nl, fwd, got, xh, xl, zh, zl, inv, back, mixed, cells, n2, ob, ps,
    load_sem, send_sem, recv_sem,
):
    me_s = lax.axis_index("space")
    me_c = lax.axis_index("chan")

    barrier = pltpu.get_barrier_semaphore()

    def greet(axis, me, size):
        def one(i, carry):
            pl.semaphore_signal(barrier, inc=1, device_id={axis: lax.rem(me + i, size)}, device_id_type=MESH)
            return carry

        lax.fori_loop(1, size, one, 0)

    greet("chan", me_c, NC)
    greet("space", me_s, NS)

    def cell_block(p):
        return pl.multiple_of(p // 4 * 16, 16), pl.multiple_of(lax.rem(p, 4) * 128, 128)

    def await_bytes(ref, sem):
        pltpu.make_async_copy(ref, ref, sem).wait()

    def send(src, dst, channel, axis, to):
        pltpu.make_async_remote_copy(
            src_ref=src,
            dst_ref=dst,
            send_sem=send_sem.at[channel],
            recv_sem=recv_sem.at[channel],
            device_id={axis: to},
            device_id_type=MESH,
        ).start()

    loads = [(field, f), (signs, sg), (lift, lf), (width, wd), (height, ht), (mlp_in, w1f), (mlp_out, w2f)]
    loads = [pltpu.make_async_copy(src, dst, load_sem.at[i]) for i, (src, dst) in enumerate(loads)]
    for load in loads:
        load.start()
    load_field, load_signs, load_lift, load_width, load_height, load_in, load_out = loads

    load_field.wait()

    def local_moments(p, carry):
        r, c = cell_block(p)
        x = f[:, pl.ds(r, 16), pl.ds(c, 128)]
        total = jnp.sum(x, axis=0)
        d = x - total * (1.0 / CL)
        part[p, 0] = total
        part[p, 1] = jnp.sum(d * d, axis=0)
        return carry

    lax.fori_loop(0, NC, local_moments, 0)
    pl.semaphore_wait(barrier, NC + NS - 2)

    def send_part(i, carry):
        p = lax.rem(me_c + i, NC)
        send(part.at[p], parts.at[me_c], 0, "chan", p)
        return carry

    lax.fori_loop(1, NC, send_part, 0)
    parts[me_c] = part[me_c]

    load_signs.wait()
    load_lift.wait()
    pick = (
        lax.broadcasted_iota(jnp.int32, (4 * BS, 2 * ROWS), 1)
        == KC * lax.broadcasted_iota(jnp.int32, (4 * BS, 2 * ROWS), 0)
    ).astype(BF16)
    spread = (
        lax.broadcasted_iota(jnp.int32, (BS, ROWS), 1) // (2 * KC)
        == lax.broadcasted_iota(jnp.int32, (BS, ROWS), 0)
    ).astype(F32)
    for b in range(NBL):
        real = exact_dot(exact_dot(lf[...], spec_one[0, b], NT), spread)
        imag = exact_dot(exact_dot(lf[...], spec_one[1, b], NT), spread)
        high, low = split(sg[0] * real + sg[1] * imag)
        m1h[b], m1l[b] = high, low
        x1h[b], x1l[b] = dot(pick, high).astype(BF16), dot(pick, low).astype(BF16)
        real = exact_dot(exact_dot(lf[:ROWS], spec_two[0, b], NT), spread)
        imag = exact_dot(exact_dot(lf[:ROWS], spec_two[1, b], NT), spread)
        high, low = split(sg[0, :ROWS] * real + sg[1, :ROWS] * imag)
        m2h[b], m2l[b] = high, low
        pick_two = pick[: 2 * BS, :ROWS]
        x2h[b], x2l[b] = dot(high, pick_two, NT).astype(BF16), dot(low, pick_two, NT).astype(BF16)

    await_bytes(parts.at[pl.ds(0, NC - 1)], recv_sem.at[0])
    totals = parts[:, 0]
    mean = jnp.sum(totals, axis=0) * (1.0 / C)
    apart = totals * (1.0 / CL) - mean
    var = (jnp.sum(parts[:, 1], axis=0) + CL * jnp.sum(apart * apart, axis=0)) * (1.0 / C)
    moments[me_c, 0] = mean
    moments[me_c, 1] = lax.rsqrt(var + 1e-05)

    def send_moments(i, carry):
        send(moments.at[me_c], moments.at[me_c], 1, "chan", lax.rem(me_c + i, NC))
        return carry

    lax.fori_loop(1, NC, send_moments, 0)

    load_in.wait()
    load_out.wait()
    w1h[...], w1l[...] = split(w1f[...] * gain_two[...])
    w2h[...], w2l[...] = split(w2f[...])
    load_width.wait()
    load_height.wait()
    await_bytes(moments.at[pl.ds(0, NC - 1)], recv_sem.at[1])

    for b in range(NBL):

        def normalise(p, carry):
            r, c = cell_block(p)
            mean, scale = moments[p, 0], moments[p, 1]
            for ch in range(BS):
                x = f[BS * b + ch, pl.ds(r, 16), pl.ds(c, 128)]
                high, low = split((x - mean) * scale * gain_one[BS * b + ch])
                row = pl.multiple_of(HL * ch + r, 16)
                nh[pl.ds(row, 16), pl.ds(c, 128)] = high
                nl[pl.ds(row, 16), pl.ds(c, 128)] = low
            return carry

        lax.fori_loop(0, NC, normalise, 0)

        def forward(j, carry):
            k = pl.multiple_of(j * 256, 256)
            table = wd[0, pl.ds(k, 256), :], wd[1, pl.ds(k, 256), :]
            y = dot3(table, (nh[...], nl[...]), NT)
            fwd[b, pl.ds(j * 8, 8)] = y.reshape(8, 2 * KC, LANES)
            return carry

        lax.fori_loop(0, 2, forward, 0)

        def send_slab(i, carry):
            p = lax.rem(me_s + i, NS)
            send(fwd.at[b, p], got.at[b, me_s], 2 + b, "space", p)
            return carry

        lax.fori_loop(1, NS, send_slab, 0)
        got[b, me_s] = fwd[b, me_s]

    column = lax.broadcasted_iota(jnp.int32, (1, KC, 256), 1)
    special = (column == 0) & (me_s == 0)
    keep = jnp.where(special, 0.0, 1.0)
    for b in range(NBL):
        await_bytes(got.at[b, pl.ds(0, NS - 1)], recv_sem.at[2 + b])

        for j in range(4):
            for g in range(2):
                tiles = swap_quarters([got[b, 4 * j + a, :, 128 * g : 128 * g + 128] for a in range(4)])
                for q in range(4):
                    high, low = split(tiles[q])
                    row = (4 * g + q) * 2 * KC
                    xh[row : row + 2 * KC, 128 * j : 128 * j + 128] = high
                    xl[row : row + 2 * KC, 128 * j : 128 * j + 128] = low

        def middle(n, carry):
            lanes = pl.ds(pl.multiple_of(256 * n, 256), 256)
            lanes_two = pl.ds(pl.multiple_of(256 * n + H, 256), 256)
            x = xh[...], xl[...]
            xc = dot3(x, (ht[0, :, lanes], ht[1, :, lanes])).reshape(BS, 2, KC, 256)
            xs = dot3(x, (ht[0, :, lanes_two], ht[1, :, lanes_two])).reshape(BS, 2, KC, 256)
            y = jnp.stack([xc[:, 0] + keep * xs[:, 1], keep * xc[:, 1] - xs[:, 0]], axis=1).reshape(ROWS, 256)
            extra = jnp.stack([xc[:, 1], -xs[:, 1]], axis=1).reshape(ROWS, 256)
            first = jnp.maximum(dot3((m1h[b], m1l[b]), split(y)), 0.0)
            m2 = m2h[b], m2l[b]
            one = shrink(dot3(m2, split(first[:ROWS]))).reshape(BS, 2, KC, 256)
            two = shrink(dot3(m2, split(first[ROWS:]))).reshape(BS, 2, KC, 256)
            real = one[:, 0] + two[:, 0]
            imag = one[:, 1] - two[:, 1]
            first = jnp.maximum(dot3((x1h[b], x1l[b]), split(extra)), 0.0)
            x2 = x2h[b], x2l[b]
            one = shrink(dot3(x2, split(first[: 2 * BS]))).reshape(BS, 2, KC, 256)
            two = shrink(dot3(x2, split(first[2 * BS :]))).reshape(BS, 2, KC, 256)
            z_real = jnp.where(special, 0.5 * (real - (one[:, 1] - two[:, 1])), real)
            z_imag = jnp.where(special, 0.5 * (imag + (one[:, 0] + two[:, 0])), imag)
            zh[:, lanes], zl[:, lanes] = split(jnp.stack([z_real, z_imag], axis=1).reshape(ROWS, 256))
            return carry

        lax.fori_loop(0, 2, middle, 0)

        def inverse(n, carry):
            lanes = pl.ds(pl.multiple_of(256 * n, 256), 256)
            lanes_two = pl.ds(pl.multiple_of(256 * n + H, 256), 256)
            z = zh[...], zl[...]
            zc = dot3(z, (ht[0, :, lanes], ht[1, :, lanes])).reshape(BS, 2, KC, 256)
            zs = dot3(z, (ht[0, :, lanes_two], ht[1, :, lanes_two])).reshape(BS, 2, KC, 256)
            o = jnp.stack([zc[:, 0] - zs[:, 1], zc[:, 1] + zs[:, 0]], axis=1).reshape(ROWS, 256)
            for j in range(2):
                for g in range(2):
                    tiles = swap_quarters(
                        [
                            o[(4 * g + q) * 2 * KC : (4 * g + q + 1) * 2 * KC, 128 * j : 128 * j + 128]
                            for q in range(4)
                        ]
                    )
                    for a in range(4):
                        inv[b, n * 8 + 4 * j + a, :, 128 * g : 128 * g + 128] = tiles[a]
            return carry

        lax.fori_loop(0, 2, inverse, 0)

        def send_rows(i, carry):
            p = lax.rem(me_s + i, NS)
            send(inv.at[b, p], back.at[b, me_s], 4 + b, "space", p)
            return carry

        lax.fori_loop(1, NS, send_rows, 0)
        back[b, me_s] = inv[b, me_s]

    me_r, me_w = cell_block(me_c)
    for b in range(NBL):
        await_bytes(back.at[b, pl.ds(0, NS - 1)], recv_sem.at[4 + b])
        nh[...], nl[...] = split(back[b].reshape(H, LANES).T)

        def residual(n, carry):
            lanes = pl.ds(pl.multiple_of(256 * n, 256), 256)
            y = dot3((nh[...], nl[...]), (wd[0, :, lanes], wd[1, :, lanes])).reshape(BS, HL, 256)
            mixed[BS * b : BS * b + BS, :, lanes] = f[BS * b : BS * b + BS, :, lanes] + y
            return carry

        lax.fori_loop(0, 2, residual, 0)

        for t in range(2):

            def send_cells(i, carry):
                p = lax.rem(me_c + i, NC)
                r, c = cell_block(p)
                send(
                    mixed.at[pl.ds(BS * b, BS), pl.ds(pl.multiple_of(r + 8 * t, 8), 8), pl.ds(c, 128)],
                    cells.at[me_c, pl.ds(BS * b, BS), pl.ds(8 * t, 8)],
                    6 + 2 * b + t,
                    "chan",
                    p,
                )
                return carry

            lax.fori_loop(1, NC, send_cells, 0)
        cells[me_c, BS * b : BS * b + BS] = mixed[BS * b : BS * b + BS, pl.ds(me_r, 16), pl.ds(me_w, 128)]

    own = []
    for t in range(2):
        for b in range(NBL):
            await_bytes(cells.at[pl.ds(0, NC - 1), pl.ds(BS * b, BS), pl.ds(8 * t, 8)], recv_sem.at[6 + 2 * b + t])
        x = cells[:, :, 8 * t : 8 * t + 8].reshape(C, 8, 128)
        mean = jnp.sum(x, axis=0) * (1.0 / C)
        d = x - mean
        scale = lax.rsqrt(jnp.sum(d * d, axis=0) * (1.0 / C) + 1e-05)
        n2[...] = (d * scale).reshape(C * 8, 128)

        def channel_mlp(j, carry):
            x = jnp.concatenate([n2[pl.ds(2 * j + i, C, stride=8), :] for i in range(2)], axis=1)
            v = dot3((w1h[...], w1l[...]), split(x))
            v = 0.5 * v * (1.0 + lax.erf(v * (2.0**-0.5)))
            y = dot3((w2h[...], w2l[...]), split(v))
            for i in range(2):
                ob[pl.ds(2 * j + i, C, stride=8), :] = y[:, 128 * i : 128 * i + 128]
            return carry

        lax.fori_loop(0, 4, channel_mlp, 0)
        ps[t] = cells[:, :, 8 * t : 8 * t + 8] + ob[...].reshape(NC, CL, 8, 128)

        rows = pl.ds(pl.multiple_of(me_r + 8 * t, 8), 8)
        place = out.at[:, rows, pl.ds(me_w, 128)]

        def send_result(i, carry):
            p = lax.rem(me_c + i, NC)
            send(ps.at[t, p], place, 10 + t, "chan", p)
            return carry

        lax.fori_loop(1, NC, send_result, 0)
        own.append(pltpu.make_async_copy(ps.at[t, me_c], place, load_sem.at[7 + t]))
        own[t].start()

    for t in range(2):
        own[t].wait()
        await_bytes(ps.at[t, pl.ds(0, NC - 1)], recv_sem.at[10 + t])

    await_bytes(part.at[pl.ds(0, NC - 1)], send_sem.at[0])
    await_bytes(parts.at[pl.ds(0, NC - 1)], send_sem.at[1])
    for b in range(NBL):
        await_bytes(fwd.at[b, pl.ds(0, NS - 1)], send_sem.at[2 + b])
        await_bytes(inv.at[b, pl.ds(0, NS - 1)], send_sem.at[4 + b])
    for t in range(2):
        for b in range(NBL):
            await_bytes(cells.at[pl.ds(0, NC - 1), pl.ds(BS * b, BS), pl.ds(8 * t, 8)], send_sem.at[6 + 2 * b + t])
        await_bytes(ps.at[t, pl.ds(0, NC - 1)], send_sem.at[10 + t])


def local(field, gain_one, spec_one, spec_two, gain_two, mlp_in, mlp_out):
    vmem = pl.BlockSpec(memory_space=pltpu.VMEM)
    smem = pl.BlockSpec(memory_space=pltpu.SMEM)
    hbm = pl.BlockSpec(memory_space=pl.ANY)
    tables = [jnp.asarray(width_table()), jnp.asarray(height_table())]
    tables += [jnp.asarray(block_signs()), jnp.asarray(channel_lift())]
    scratch = [
        ((CL, HL, H), F32),
        ((2, H, H), BF16),
        ((2, H, 2 * H), BF16),
        ((2, 2 * ROWS, ROWS), F32),
        ((2 * ROWS, BS), F32),
        ((HID, C), F32),
        ((C, HID), F32),
        ((HID, C), BF16),
        ((HID, C), BF16),
        ((C, HID), BF16),
        ((C, HID), BF16),
        ((NBL, 2 * ROWS, ROWS), BF16),
        ((NBL, 2 * ROWS, ROWS), BF16),
        ((NBL, ROWS, ROWS), BF16),
        ((NBL, ROWS, ROWS), BF16),
        ((NBL, 4 * BS, ROWS), BF16),
        ((NBL, 4 * BS, ROWS), BF16),
        ((NBL, ROWS, 2 * BS), BF16),
        ((NBL, ROWS, 2 * BS), BF16),
        ((NC, 2, 16, 128), F32),
        ((NC, 2, 16, 128), F32),
        ((NC, 2, 16, 128), F32),
        ((LANES, H), BF16),
        ((LANES, H), BF16),
        ((NBL, NS, 2 * KC, LANES), F32),
        ((NBL, NS, 2 * KC, LANES), F32),
        ((ROWS, H), BF16),
        ((ROWS, H), BF16),
        ((ROWS, H), BF16),
        ((ROWS, H), BF16),
        ((NBL, NS, 2 * KC, LANES), F32),
        ((NBL, NS, 2 * KC, LANES), F32),
        ((CL, HL, H), F32),
        ((NC, CL, 16, 128), F32),
        ((C * 8, 128), F32),
        ((C * 8, 128), F32),
        ((2, NC, CL, 8, 128), F32),
    ]
    return pl.pallas_call(
        kernel,
        out_shape=jax.ShapeDtypeStruct((CL, HL, H), F32),
        in_specs=[smem, vmem, vmem, vmem] + [hbm] * 7,
        out_specs=hbm,
        scratch_shapes=[pltpu.VMEM(shape, dtype) for shape, dtype in scratch]
        + [pltpu.SemaphoreType.DMA((9,)), pltpu.SemaphoreType.DMA((12,)), pltpu.SemaphoreType.DMA((12,))],
        compiler_params=pltpu.CompilerParams(
            collective_id=0, has_side_effects=True, vmem_limit_bytes=56 * 1024 * 1024
        ),
        name="afno_block",
    )(gain_one, spec_one, spec_two, gain_two.reshape(1, C), field, mlp_in, mlp_out, *tables)


def solution(mesh):
    placed = (
        P("chan", "space", None),
        P("chan"),
        P(None, "chan", None, None),
        P(None, "chan", None, None),
        P(),
        P(),
        P(),
    )
    return jax.shard_map(
        local, mesh=mesh, in_specs=placed, out_specs=P("chan", "space", None), check_vma=False
    )
```

```python
import functools

import jax
import jax.numpy as jnp
import ml_dtypes
import numpy as np
from jax import lax
from jax.experimental import pallas as pl
from jax.experimental.pallas import tpu as pltpu
from jax.sharding import PartitionSpec as P

MESH = pl.DeviceIdType.MESH
F32 = jnp.float32
BF16 = jnp.bfloat16

H = 512
C = 128
HID = 512
NS = 16
NC = 8
CL = C // NC
HL = H // NS
BS = 8
NBL = CL // BS
KC = 16
ROWS = BS * 2 * KC
LANES = BS * HL
HALF = H // 2

NN = ((1,), (0,))
NT = ((1,), (1,))


def halves(table):
    high = table.astype(ml_dtypes.bfloat16)
    low = (table - high.astype(np.float64)).astype(ml_dtypes.bfloat16)
    return np.stack([high, low])


def width_table():
    row = np.arange(HALF)
    number = (row // (2 * KC)) * KC + row % KC
    imag = (row // KC) % 2 == 1
    both = []
    for odd in (0, 1):
        nyquist = imag & (number == 0) & (odd == 0)
        freq = np.where(nyquist, H // 2, 2 * number + odd)
        angle = 2 * np.pi / H * (freq[:, None] * np.arange(HALF)[None, :] % H)
        both.append(np.where((imag & ~nyquist)[:, None], -np.sin(angle), np.cos(angle)) / np.sqrt(H))
    return halves(np.stack(both))


def height_table():
    series = np.arange(HALF)
    ways = []
    for odd in (0, 1):
        angle = 2 * np.pi / H * (series[:, None] * (2 * series + odd)[None, :] % H)
        ways.append((np.cos(angle), np.sin(angle)))
    there = np.stack([np.concatenate([c, s], axis=1) for c, s in ways])
    back = np.stack([np.concatenate([c.T, s.T], axis=1) for c, s in ways])
    return halves(np.stack([there, back]) / np.sqrt(H))


def split(x):
    high = x.astype(BF16)
    return high, (x - high.astype(F32)).astype(BF16)


def dot(a, b, dims=NN):
    return lax.dot_general(a, b, (dims, ((), ())), preferred_element_type=F32)


def dot3(a, b, dims=NN):
    left = jnp.concatenate([a[0], a[0], a[1]], axis=dims[0][0])
    right = jnp.concatenate([b[0], b[1], b[0]], axis=dims[1][0])
    return dot(left, right, dims)


def exact_dot(a, b, dims=NN):
    return lax.dot_general(a, b, (dims, ((), ())), precision=lax.Precision.HIGHEST, preferred_element_type=F32)


def iota(shape, axis):
    return lax.broadcasted_iota(jnp.int32, shape, axis)


def gelu(v):
    return 0.5 * v * (1.0 + lax.erf(v * 2.0**-0.5))


def shrink(v):
    return jnp.maximum(v - 0.01, 0.0) + jnp.minimum(v + 0.01, 0.0)


def swap_quarters(t):
    lane = lax.broadcasted_iota(jnp.int32, t[0].shape, 1)
    low = lane < 64
    even = lane % 64 < 32
    u0 = jnp.where(low, t[0], pltpu.roll(t[2], 64, 1))
    u2 = jnp.where(low, pltpu.roll(t[0], 64, 1), t[2])
    u1 = jnp.where(low, t[1], pltpu.roll(t[3], 64, 1))
    u3 = jnp.where(low, pltpu.roll(t[1], 64, 1), t[3])
    v0 = jnp.where(even, u0, pltpu.roll(u1, 32, 1))
    v1 = jnp.where(even, pltpu.roll(u0, 96, 1), u1)
    v2 = jnp.where(even, u2, pltpu.roll(u3, 32, 1))
    v3 = jnp.where(even, pltpu.roll(u2, 96, 1), u3)
    return v0, v1, v2, v3


def kernel(
    gain_one, spec_one, spec_two, gain_two, field, mlp_in, mlp_out, width, height, out,
    f, wd, ht, w1f, w2f, w1h, w1l, w2h, w2l, rw, m1h, m1l, m2h, m2l, x1h, x1l, x2h, x2l,
    part, parts, moments, nh, nl, fwd, got, xh, xl, zh, zl, inv, back, mixed, cells, n2, ob, ps,
    load_sem, send_sem, recv_sem,
):
    me_s = lax.axis_index("space")
    me_c = lax.axis_index("chan")

    loads = [(field.at[:, pl.ds(16 * i, 16)], f.at[:, pl.ds(16 * i, 16)]) for i in range(2)]
    loads += [(width, wd), (height, ht), (mlp_in, w1f), (mlp_out, w2f)]
    loads = [pltpu.make_async_copy(src, dst, load_sem.at[i]) for i, (src, dst) in enumerate(loads)]
    for load in loads:
        load.start()
    load_width, load_height, load_in, load_out = loads[2:]

    barrier = pltpu.get_barrier_semaphore()

    def greet(axis, me, size):
        def one(i, carry):
            pl.semaphore_signal(barrier, inc=1, device_id={axis: lax.rem(me + i, size)}, device_id_type=MESH)
            return carry

        lax.fori_loop(1, size, one, 0)

    greet("chan", me_c, NC)
    greet("space", me_s, NS)

    def cell_block(p):
        return pl.multiple_of(p // 4 * 16, 16), pl.multiple_of(lax.rem(p, 4) * 128, 128)

    def arrive(ref, channel):
        pltpu.make_async_copy(ref, ref, recv_sem.at[channel]).wait()

    def leave(ref, channel):
        pltpu.make_async_copy(ref, ref, send_sem.at[channel]).wait()

    def send(src, dst, channel, axis, to):
        pltpu.make_async_remote_copy(
            src_ref=src,
            dst_ref=dst,
            send_sem=send_sem.at[channel],
            recv_sem=recv_sem.at[channel],
            device_id={axis: to},
            device_id_type=MESH,
        ).start()

    def local_moments(p, carry):
        r, c = cell_block(p)
        x = f[:, pl.ds(r, 16), pl.ds(c, 128)]
        total = jnp.sum(x, axis=0)
        d = x - total * (1.0 / CL)
        part[p, 0] = total
        part[p, 1] = jnp.sum(d * d, axis=0)
        return carry

    for i in range(2):
        loads[i].wait()
        lax.fori_loop(4 * i, 4 * i + 4, local_moments, 0)
    pl.semaphore_wait(barrier, NC + NS - 2)

    def send_part(i, carry):
        p = lax.rem(me_c + i, NC)
        send(part.at[p], parts.at[me_c], 0, "chan", p)
        return carry

    lax.fori_loop(1, NC, send_part, 0)
    parts[me_c] = part[me_c]

    lift = jnp.concatenate(
        [
            iota((4 * BS, BS), 0) // 2 % BS == iota((4 * BS, BS), 1),
            iota((4 * BS, BS), 0) % BS == iota((4 * BS, BS), 1),
        ],
        axis=0,
    ).astype(F32)
    weights = jnp.concatenate([spec_one[...].reshape(4 * BS, BS), spec_two[...].reshape(4 * BS, BS)], axis=0)
    lifted = exact_dot(lift, weights, NT)
    high = lifted.astype(BF16)
    rest = lifted - high.astype(F32)
    middle_term = rest.astype(BF16)
    low = (rest - middle_term.astype(F32)).astype(BF16)
    wide = (iota((8 * BS, 8 * ROWS), 1) // (2 * KC) == iota((8 * BS, 8 * ROWS), 0)).astype(BF16)
    lane = iota((8 * BS, 8 * 128), 1)
    slim = ((lane // 128 * BS + lane % BS == iota((8 * BS, 8 * 128), 0)) & (lane % 128 < 2 * BS)).astype(BF16)

    def spread(rows, table):
        terms = jnp.concatenate([high[rows], middle_term[rows], low[rows]], axis=0)
        terms = dot(terms, table)
        return terms[: 4 * BS] + (terms[4 * BS : 8 * BS] + terms[8 * BS :])

    def complex_form(values, width, part_out, part_in, layer, b):
        variant = iota((4 * BS, width), 0) // (2 * BS)
        real = values[:, (4 * layer + b) * width : (4 * layer + b + 1) * width]
        imag = values[:, (4 * layer + 2 + b) * width : (4 * layer + 2 + b + 1) * width]
        real = jnp.where((variant == 1) & (part_out == 1), -real, real)
        imag = jnp.where((variant == 0) & (part_out == 0), -imag, imag)
        return jnp.where(part_out == part_in, real, imag)

    big = spread(slice(0, 4 * BS), wide)
    small = spread(slice(4 * BS, 8 * BS), slim)
    same_column = iota((KC, ROWS), 1) % KC == iota((KC, ROWS), 0)
    for b in range(NBL):
        for layer in range(2):
            part_out, part_in = iota((4 * BS, ROWS), 0) % 2, iota((4 * BS, ROWS), 1) // KC % 2
            rw[2 * b + layer] = complex_form(big, ROWS, part_out, part_in, layer, b)
            for r in range(4 * BS if layer == 0 else 2 * BS):
                row_high, row_low = split(jnp.where(same_column, rw[2 * b + layer, r : r + 1, :], 0.0))
                to_high, to_low = ((m1h, m1l), (m2h, m2l))[layer]
                to_high[b, KC * r : KC * r + KC] = row_high
                to_low[b, KC * r : KC * r + KC] = row_low
            part_out, part_in = iota((4 * BS, 128), 0) // BS % 2, iota((4 * BS, 128), 1) // BS % 2
            form = complex_form(small, 128, part_out, part_in, layer, b)
            if layer == 0:
                x1h[b], x1l[b] = split(form)
            else:
                x2h[b], x2l[b] = split(form[: 2 * BS])

    arrive(parts.at[pl.ds(0, NC - 1)], 0)
    totals = parts[:, 0]
    mean = jnp.sum(totals, axis=0) * (1.0 / C)
    apart = totals * (1.0 / CL) - mean
    var = (jnp.sum(parts[:, 1], axis=0) + CL * jnp.sum(apart * apart, axis=0)) * (1.0 / C)
    moments[me_c, 0] = mean
    moments[me_c, 1] = lax.rsqrt(var + 1e-05)

    def send_moments(i, carry):
        send(moments.at[me_c], moments.at[me_c], 1, "chan", lax.rem(me_c + i, NC))
        return carry

    lax.fori_loop(1, NC, send_moments, 0)

    load_in.wait()
    load_out.wait()
    w1h[...], w1l[...] = split(w1f[...] * gain_two[...])
    w2h[...], w2l[...] = split(w2f[...])
    load_width.wait()
    load_height.wait()
    arrive(moments.at[pl.ds(0, NC - 1)], 1)

    for b in range(NBL):

        for i in range(4):
            p = 4 * (i // 2) + i % 2
            r, c = i // 2 * 16, i % 2 * 128
            mean, scale = moments[p, 0], moments[p, 1]
            mean_two, scale_two = moments[p + 2, 0], moments[p + 2, 1]
            for ch in range(BS):
                x = (f[BS * b + ch, r : r + 16, c : c + 128] - mean) * scale
                x_two = (f[BS * b + ch, r : r + 16, HALF + c : HALF + c + 128] - mean_two) * scale_two
                x, x_two = x * gain_one[BS * b + ch], x_two * gain_one[BS * b + ch]
                rows, lanes = slice(HL * ch + r, HL * ch + r + 16), slice(c, c + 128)
                nh[0, rows, lanes], nl[0, rows, lanes] = split(x + x_two)
                nh[1, rows, lanes], nl[1, rows, lanes] = split(x - x_two)

        for j in range(2):
            y = dot3((wd[0, j], wd[1, j]), (nh[j], nl[j]), NT)
            fwd[b, 8 * j : 8 * j + 8] = y.reshape(8, 2 * KC, LANES)

        def send_slab(i, carry):
            p = lax.rem(me_s + i, NS)
            send(fwd.at[b, p], got.at[b, me_s], 2 + b, "space", p)
            return carry

        lax.fori_loop(1, NS, send_slab, 0)
        got[b, me_s] = fwd[b, me_s]

    special = (iota((KC, H), 0) == 0) & (me_s == 0)
    keep = jnp.where(special, 0.0, 1.0)
    for b in range(NBL):
        arrive(got.at[b, pl.ds(0, NS - 1)], 2 + b)

        for j in range(2):
            for g in range(2):
                lanes = slice(128 * g, 128 * g + 128)
                tiles = swap_quarters([got[b, 4 * j + a, :, lanes] for a in range(4)])
                tiles_two = swap_quarters([got[b, 4 * (j + 2) + a, :, lanes] for a in range(4)])
                for q in range(4):
                    rows = slice((4 * g + q) * 2 * KC, (4 * g + q + 1) * 2 * KC)
                    to = slice(128 * j, 128 * j + 128)
                    xh[0, rows, to], xl[0, rows, to] = split(tiles[q] + tiles_two[q])
                    xh[1, rows, to], xl[1, rows, to] = split(tiles[q] - tiles_two[q])

        both = []
        for n in range(2):
            x = dot3((xh[n], xl[n]), (ht[0, 0, n], ht[1, 0, n]))
            both.append((x[:, :HALF], x[:, HALF:]))
        xc, xs = (jnp.concatenate(pair, axis=1).reshape(BS, 2, KC, H) for pair in zip(*both))
        y = jnp.stack([xc[:, 0] + keep * xs[:, 1], keep * xc[:, 1] - xs[:, 0]], axis=1).reshape(ROWS, H)
        first = jnp.maximum(dot3((m1h[b], m1l[b]), split(y)), 0.0)
        m2 = m2h[b], m2l[b]
        one = shrink(dot3(m2, split(first[:ROWS]))).reshape(BS, 2, KC, H)
        two = shrink(dot3(m2, split(first[ROWS:]))).reshape(BS, 2, KC, H)
        real = one[:, 0] + two[:, 0]
        imag = one[:, 1] - two[:, 1]
        channel = iota((BS, H), 0)
        extra_real, extra_imag = jnp.zeros((BS, H), F32), jnp.zeros((BS, H), F32)
        for ch in range(BS):
            extra_real = jnp.where(channel == ch, xc[ch, 1, 0:1], extra_real)
            extra_imag = jnp.where(channel == ch, -xs[ch, 1, 0:1], extra_imag)
        extra = jnp.concatenate([extra_real, extra_imag], axis=0)
        first = jnp.maximum(dot3((x1h[b, :, : 2 * BS], x1l[b, :, : 2 * BS]), split(extra)), 0.0)
        x2 = x2h[b, :, : 2 * BS], x2l[b, :, : 2 * BS]
        one = shrink(dot3(x2, split(first[: 2 * BS])))
        two = shrink(dot3(x2, split(first[2 * BS :])))
        extra_real = one[:BS] + two[:BS]
        extra_imag = one[BS:] - two[BS:]
        for ch in range(BS):
            z_real = jnp.where(special, 0.5 * (real[ch] - extra_imag[ch : ch + 1]), real[ch])
            z_imag = jnp.where(special, 0.5 * (imag[ch] + extra_real[ch : ch + 1]), imag[ch])
            for i, z in enumerate((z_real, z_imag)):
                rows = slice((2 * ch + i) * KC, (2 * ch + i + 1) * KC)
                for n in range(2):
                    zh[n, rows], zl[n, rows] = split(z[:, HALF * n : HALF * n + HALF])

        halves_of = []
        for n in range(2):
            z = dot3((zh[n], zl[n]), (ht[0, 1, n], ht[1, 1, n]))
            zc = z[:, :HALF].reshape(BS, 2, KC, HALF)
            zs = z[:, HALF:].reshape(BS, 2, KC, HALF)
            halves_of.append(jnp.stack([zc[:, 0] - zs[:, 1], zc[:, 1] + zs[:, 0]], axis=1).reshape(ROWS, HALF))
        halves_of = halves_of[0] + halves_of[1], halves_of[0] - halves_of[1]
        for j in range(4):
            for g in range(2):
                lanes = slice(128 * (j % 2), 128 * (j % 2) + 128)
                rows = [slice((4 * g + q) * 2 * KC, (4 * g + q + 1) * 2 * KC) for q in range(4)]
                tiles = swap_quarters([halves_of[j // 2][rows[q], lanes] for q in range(4)])
                for a in range(4):
                    inv[b, 4 * j + a, :, 128 * g : 128 * g + 128] = tiles[a]

        def send_rows(i, carry):
            p = lax.rem(me_s + i, NS)
            send(inv.at[b, p], back.at[b, me_s], 4 + b, "space", p)
            return carry

        lax.fori_loop(1, NS, send_rows, 0)
        back[b, me_s] = inv[b, me_s]

    me_r, me_w = cell_block(me_c)
    for b in range(NBL):
        arrive(back.at[b, pl.ds(0, NS - 1)], 4 + b)
        channels = slice(BS * b, BS * b + BS)
        sums = []
        for j in range(2):
            columns = split(back[b, 8 * j : 8 * j + 8].reshape(HALF, LANES).T)
            sums.append(dot3(columns, (wd[0, j], wd[1, j])))
        mixed[channels, :, :HALF] = f[channels, :, :HALF] + (sums[0] + sums[1]).reshape(BS, HL, HALF)
        mixed[channels, :, HALF:] = f[channels, :, HALF:] + (sums[0] - sums[1]).reshape(BS, HL, HALF)

        for t in range(2):

            def send_cells(i, carry):
                p = lax.rem(me_c + i, NC)
                r, c = cell_block(p)
                send(
                    mixed.at[pl.ds(BS * b, BS), pl.ds(pl.multiple_of(r + 8 * t, 8), 8), pl.ds(c, 128)],
                    cells.at[me_c, pl.ds(BS * b, BS), pl.ds(8 * t, 8)],
                    6 + 2 * b + t,
                    "chan",
                    p,
                )
                return carry

            lax.fori_loop(1, NC, send_cells, 0)
        cells[me_c, BS * b : BS * b + BS] = mixed[BS * b : BS * b + BS, pl.ds(me_r, 16), pl.ds(me_w, 128)]

    own = []
    for t in range(2):
        for b in range(NBL):
            arrive(cells.at[pl.ds(0, NC - 1), pl.ds(BS * b, BS), pl.ds(8 * t, 8)], 6 + 2 * b + t)
        x = cells[:, :, 8 * t : 8 * t + 8].reshape(C, 8, 128)
        mean = jnp.sum(x, axis=0) * (1.0 / C)
        d = x - mean
        scale = lax.rsqrt(jnp.sum(d * d, axis=0) * (1.0 / C) + 1e-05)
        n2[...] = (d * scale).reshape(C * 8, 128)

        x = jnp.concatenate([n2[pl.ds(i, C, stride=8), :] for i in range(8)], axis=1)
        v = gelu(dot3((w1h[...], w1l[...]), split(x)))
        y = dot3((w2h[...], w2l[...]), split(v))
        for i in range(8):
            ob[pl.ds(i, C, stride=8), :] = y[:, 128 * i : 128 * i + 128]
        ps[t] = cells[:, :, 8 * t : 8 * t + 8] + ob[...].reshape(NC, CL, 8, 128)

        rows = pl.ds(pl.multiple_of(me_r + 8 * t, 8), 8)
        place = out.at[:, rows, pl.ds(me_w, 128)]

        def send_result(i, carry):
            p = lax.rem(me_c + i, NC)
            send(ps.at[t, p], place, 10 + t, "chan", p)
            return carry

        lax.fori_loop(1, NC, send_result, 0)
        own.append(pltpu.make_async_copy(ps.at[t, me_c], place, load_sem.at[6 + t]))
        own[t].start()

    for t in range(2):
        own[t].wait()
        arrive(ps.at[t, pl.ds(0, NC - 1)], 10 + t)

    leave(part.at[pl.ds(0, NC - 1)], 0)
    leave(parts.at[pl.ds(0, NC - 1)], 1)
    for b in range(NBL):
        leave(fwd.at[b, pl.ds(0, NS - 1)], 2 + b)
        leave(inv.at[b, pl.ds(0, NS - 1)], 4 + b)
    for t in range(2):
        for b in range(NBL):
            leave(cells.at[pl.ds(0, NC - 1), pl.ds(BS * b, BS), pl.ds(8 * t, 8)], 6 + 2 * b + t)
        leave(ps.at[t, pl.ds(0, NC - 1)], 10 + t)


def local(field, gain_one, spec_one, spec_two, gain_two, mlp_in, mlp_out):
    vmem = pl.BlockSpec(memory_space=pltpu.VMEM)
    smem = pl.BlockSpec(memory_space=pltpu.SMEM)
    hbm = pl.BlockSpec(memory_space=pl.ANY)
    tables = [jnp.asarray(width_table()), jnp.asarray(height_table())]
    scratch = [
        ((CL, HL, H), F32),
        ((2, 2, HALF, HALF), BF16),
        ((2, 2, 2, HALF, H), BF16),
        ((HID, C), F32),
        ((C, HID), F32),
        ((HID, C), BF16),
        ((HID, C), BF16),
        ((C, HID), BF16),
        ((C, HID), BF16),
        ((2 * NBL, 4 * BS, ROWS), F32),
        ((NBL, 2 * ROWS, ROWS), BF16),
        ((NBL, 2 * ROWS, ROWS), BF16),
        ((NBL, ROWS, ROWS), BF16),
        ((NBL, ROWS, ROWS), BF16),
        ((NBL, 4 * BS, 128), BF16),
        ((NBL, 4 * BS, 128), BF16),
        ((NBL, 2 * BS, 128), BF16),
        ((NBL, 2 * BS, 128), BF16),
        ((NC, 2, 16, 128), F32),
        ((NC, 2, 16, 128), F32),
        ((NC, 2, 16, 128), F32),
        ((2, LANES, HALF), BF16),
        ((2, LANES, HALF), BF16),
        ((NBL, NS, 2 * KC, LANES), F32),
        ((NBL, NS, 2 * KC, LANES), F32),
        ((2, ROWS, HALF), BF16),
        ((2, ROWS, HALF), BF16),
        ((2, ROWS, HALF), BF16),
        ((2, ROWS, HALF), BF16),
        ((NBL, NS, 2 * KC, LANES), F32),
        ((NBL, NS, 2 * KC, LANES), F32),
        ((CL, HL, H), F32),
        ((NC, CL, 16, 128), F32),
        ((C * 8, 128), F32),
        ((C * 8, 128), F32),
        ((2, NC, CL, 8, 128), F32),
    ]
    return pl.pallas_call(
        kernel,
        out_shape=pltpu.VMEM((CL, HL, H), F32),
        in_specs=[smem, vmem, vmem, vmem] + [hbm] * 5,
        out_specs=pl.BlockSpec(memory_space=pltpu.VMEM),
        scratch_shapes=[pltpu.VMEM(shape, dtype) for shape, dtype in scratch]
        + [pltpu.SemaphoreType.DMA((8,)), pltpu.SemaphoreType.DMA((12,)), pltpu.SemaphoreType.DMA((12,))],
        compiler_params=pltpu.CompilerParams(
            collective_id=0, has_side_effects=True, vmem_limit_bytes=56 * 1024 * 1024
        ),
        name="afno_block",
    )(gain_one, spec_one, spec_two, gain_two.reshape(1, C), field, mlp_in, mlp_out, *tables)


def solution(mesh):
    placed = (
        P("chan", "space", None),
        P("chan"),
        P(None, "chan", None, None),
        P(None, "chan", None, None),
        P(),
        P(),
        P(),
    )
    return jax.shard_map(
        local, mesh=mesh, in_specs=placed, out_specs=P("chan", "space", None), check_vma=False
    )
```

```python
import functools

import jax
import jax.numpy as jnp
import ml_dtypes
import numpy as np
from jax import lax
from jax.experimental import pallas as pl
from jax.experimental.pallas import tpu as pltpu
from jax.sharding import PartitionSpec as P

MESH = pl.DeviceIdType.MESH
F32 = jnp.float32
BF16 = jnp.bfloat16

H = 512
C = 128
HID = 512
NS = 16
NC = 8
CL = C // NC
HL = H // NS
BS = 8
NBL = CL // BS
KC = 16
ROWS = BS * 2 * KC
HALF = H // 2
HH = HL // 2

NN = ((1,), (0,))
NT = ((1,), (1,))


def halves(table):
    high = table.astype(ml_dtypes.bfloat16)
    low = (table - high.astype(np.float64)).astype(ml_dtypes.bfloat16)
    return np.stack([high, low])


def width_table():
    row = np.arange(HALF)
    number = (row // (2 * KC)) * KC + row % KC
    imag = (row // KC) % 2 == 1
    both = []
    for odd in (0, 1):
        nyquist = imag & (number == 0) & (odd == 0)
        freq = np.where(nyquist, H // 2, 2 * number + odd)
        angle = 2 * np.pi / H * (freq[:, None] * np.arange(HALF)[None, :] % H)
        both.append(np.where((imag & ~nyquist)[:, None], -np.sin(angle), np.cos(angle)) / np.sqrt(H))
    return halves(np.stack(both))


def height_table():
    index = np.arange(HALF)
    h = index % 128 // HH * HL + index // 128 * HH + index % HH
    there, back = [], []
    for odd in (0, 1):
        angle = 2 * np.pi / H * (h[:, None] * (2 * index + odd)[None, :] % H)
        cosine, sine = np.cos(angle) / np.sqrt(H), np.sin(angle) / np.sqrt(H)
        there.append(np.concatenate([cosine, sine], axis=1))
        back.append(np.stack([np.concatenate([cosine.T[:, k], sine.T[:, k]], axis=1) for k in np.split(index, 2)]))
    return halves(np.stack(there)), halves(np.stack(back))


def split(x):
    high = x.astype(BF16)
    return high, (x - high.astype(F32)).astype(BF16)


def dot(a, b, dims=NN):
    return lax.dot_general(a, b, (dims, ((), ())), preferred_element_type=F32)


def dot3(a, b, dims=NN):
    left = jnp.concatenate([a[0], a[0], a[1]], axis=dims[0][0])
    right = jnp.concatenate([b[0], b[1], b[0]], axis=dims[1][0])
    return dot(left, right, dims)


def exact_dot(a, b, dims=NN):
    return lax.dot_general(a, b, (dims, ((), ())), precision=lax.Precision.HIGHEST, preferred_element_type=F32)


def iota(shape, axis):
    return lax.broadcasted_iota(jnp.int32, shape, axis)


def gelu(v):
    return 0.5 * v * (1.0 + lax.erf(v * 2.0**-0.5))


def shrink(v):
    return jnp.maximum(v - 0.01, 0.0) + jnp.minimum(v + 0.01, 0.0)


def swap_eighths(tiles):
    tiles = list(tiles)
    lane = iota(tiles[0].shape, 1)
    for step in (4, 2, 1):
        width = 16 * step
        low = lane // width % 2 == 0
        for i in range(8):
            if i & step == 0:
                one, two = tiles[i], tiles[i + step]
                tiles[i] = jnp.where(low, one, pltpu.roll(two, width, 1))
                tiles[i + step] = jnp.where(low, pltpu.roll(one, 128 - width, 1), two)
    return tiles


def kernel(
    gain_one, spec_one, spec_two, gain_two, field, mlp_in, mlp_out, width, there, here, out,
    f, wd, ht, hb, w1f, w2f, w1h, w1l, w2h, w2l, rw, m1h, m1l, m2h, m2l, x1h, x1l, x2h, x2l,
    part, parts, moments, nh, nl, fwd, got, xh, xl, zh, zl, inv, back, mixed, cells, n2, ob, ps,
    load_sem, send_sem, recv_sem,
):
    me_s = lax.axis_index("space")
    me_c = lax.axis_index("chan")

    loads = [(field.at[:, pl.ds(16 * i, 16)], f.at[:, pl.ds(16 * i, 16)]) for i in range(2)]
    loads += [(width, wd), (there, ht), (here, hb), (mlp_in, w1f), (mlp_out, w2f)]
    loads = [pltpu.make_async_copy(src, dst, load_sem.at[i]) for i, (src, dst) in enumerate(loads)]
    for load in loads[:2]:
        load.start()
    load_width, load_there, load_here, load_in, load_out = loads[2:]

    barrier = pltpu.get_barrier_semaphore()

    def greet(axis, me, size):
        def one(i, carry):
            pl.semaphore_signal(barrier, inc=1, device_id={axis: lax.rem(me + i, size)}, device_id_type=MESH)
            return carry

        lax.fori_loop(1, size, one, 0)

    greet("chan", me_c, NC)
    greet("space", me_s, NS)

    def cell_block(p, t):
        return (
            pl.ds(pl.multiple_of(t * HH + p // 4 * 8, 8), 8),
            pl.ds(pl.multiple_of(lax.rem(p, 4) * 128, 128), 128),
        )

    flight = {}

    def arrive(ref, channel):
        pltpu.make_async_copy(ref, ref, recv_sem.at[channel]).wait()

    def leave(channel):
        ref = flight.pop(channel)
        pltpu.make_async_copy(ref, ref, send_sem.at[channel]).wait()

    def send_all(channel, axis, pair):
        me, size = (me_c, NC) if axis == "chan" else (me_s, NS)

        def one(i, carry):
            if axis == "chan":
                p = lax.rem(me // 2 + i // 2 + 2, 4) * 2 + lax.rem(me + i, 2)
            else:
                p = lax.rem(me // 4 + i // 4 + 2, 4) * 4 + lax.rem(me + i + 2, 4)
            src, dst = pair(p)
            pltpu.make_async_remote_copy(
                src_ref=src,
                dst_ref=dst,
                send_sem=send_sem.at[channel],
                recv_sem=recv_sem.at[channel],
                device_id={axis: p},
                device_id_type=MESH,
            ).start()
            return carry

        own = 4 if axis == "chan" else 10
        lax.fori_loop(0, own, one, 0)
        lax.fori_loop(own + 1, size, one, 0)

    for t in range(2):
        loads[t].wait()

        for p in range(NC):
            r, c = HH * t + 8 * (p // 4), 128 * (p % 4)
            x = f[:, r : r + 8, c : c + 128]
            total = jnp.sum(x, axis=0)
            d = x - total * (1.0 / CL)
            part[t, p, 0] = total
            part[t, p, 1] = jnp.sum(d * d, axis=0)
    for load in loads[2:]:
        load.start()
    pl.semaphore_wait(barrier, NC + NS - 2)
    for t in range(2):
        send_all(t, "chan", lambda p: (part.at[t, p], parts.at[t, me_c]))
        flight[t] = part.at[t, pl.ds(0, NC - 1)]
        parts[t, me_c] = part[t, me_c]

    lift = jnp.concatenate(
        [
            iota((4 * BS, BS), 0) // 2 % BS == iota((4 * BS, BS), 1),
            iota((4 * BS, BS), 0) % BS == iota((4 * BS, BS), 1),
        ],
        axis=0,
    ).astype(F32)
    weights = jnp.concatenate([spec_one[...].reshape(4 * BS, BS), spec_two[...].reshape(4 * BS, BS)], axis=0)
    lifted = exact_dot(lift, weights, NT)
    high = lifted.astype(BF16)
    rest = lifted - high.astype(F32)
    middle_term = rest.astype(BF16)
    low = (rest - middle_term.astype(F32)).astype(BF16)
    wide = (iota((8 * BS, 8 * ROWS), 1) // (2 * KC) == iota((8 * BS, 8 * ROWS), 0)).astype(BF16)
    lane = iota((8 * BS, 8 * 128), 1)
    slim = ((lane // 128 * BS + lane % BS == iota((8 * BS, 8 * 128), 0)) & (lane % 128 < 2 * BS)).astype(BF16)

    def spread(rows, table):
        terms = jnp.concatenate([high[rows], middle_term[rows], low[rows]], axis=0)
        terms = dot(terms, table)
        return terms[: 4 * BS] + (terms[4 * BS : 8 * BS] + terms[8 * BS :])

    def complex_form(values, width, part_out, part_in, layer, b):
        variant = iota((4 * BS, width), 0) // (2 * BS)
        real = values[:, (4 * layer + b) * width : (4 * layer + b + 1) * width]
        imag = values[:, (4 * layer + 2 + b) * width : (4 * layer + 2 + b + 1) * width]
        real = jnp.where((variant == 1) & (part_out == 1), -real, real)
        imag = jnp.where((variant == 0) & (part_out == 0), -imag, imag)
        return jnp.where(part_out == part_in, real, imag)

    big = spread(slice(0, 4 * BS), wide)
    small = spread(slice(4 * BS, 8 * BS), slim)
    same_column = iota((KC, ROWS), 1) % KC == iota((KC, ROWS), 0)
    for b in range(NBL):
        for layer in range(2):
            part_out, part_in = iota((4 * BS, ROWS), 0) % 2, iota((4 * BS, ROWS), 1) // KC % 2
            rw[2 * b + layer] = complex_form(big, ROWS, part_out, part_in, layer, b)
            for r in range(4 * BS if layer == 0 else 2 * BS):
                row_high, row_low = split(jnp.where(same_column, rw[2 * b + layer, r : r + 1, :], 0.0))
                to_high, to_low = ((m1h, m1l), (m2h, m2l))[layer]
                to_high[b, KC * r : KC * r + KC] = row_high
                to_low[b, KC * r : KC * r + KC] = row_low
            part_out, part_in = iota((4 * BS, 128), 0) // BS % 2, iota((4 * BS, 128), 1) // BS % 2
            form = complex_form(small, 128, part_out, part_in, layer, b)
            if layer == 0:
                x1h[b], x1l[b] = split(form)
            else:
                x2h[b], x2l[b] = split(form[: 2 * BS])

    for t in range(2):
        arrive(parts.at[t, pl.ds(0, NC - 1)], t)
        totals = parts[t, :, 0]
        mean = jnp.sum(totals, axis=0) * (1.0 / C)
        apart = totals * (1.0 / CL) - mean
        var = (jnp.sum(parts[t, :, 1], axis=0) + CL * jnp.sum(apart * apart, axis=0)) * (1.0 / C)
        moments[t, me_c, 0] = mean
        moments[t, me_c, 1] = lax.rsqrt(var + 1e-05)

        send_all(2 + t, "chan", lambda p: (moments.at[t, me_c], moments.at[t, me_c]))
        flight[2 + t] = moments.at[t, pl.ds(0, NC - 1)]

    load_in.wait()
    load_out.wait()
    w1h[...], w1l[...] = split(w1f[...] * gain_two[...])
    w2h[...], w2l[...] = split(w2f[...])
    load_width.wait()

    def send_slab(t, b):
        channel = 4 + 2 * t + b
        send_all(channel, "space", lambda p: (fwd.at[t, b, p], got.at[t, b, me_s]))
        flight[channel] = fwd.at[t, b, pl.ds(0, NS - 1)]
        got[t, b, me_s] = fwd[t, b, me_s]

    for t in range(2):
        arrive(moments.at[t, pl.ds(0, NC - 1)], 2 + t)
        for i in range(2):
            both = []
            for k in (i, i + 2):
                both.append([jnp.concatenate([moments[t, k, m], moments[t, k + 4, m]], axis=0) for m in range(2)])
            for ch in range(CL):
                x, x_two = (
                    (f[ch, HH * t : HH * t + HH, c : c + 128] - mean) * scale * gain_one[ch]
                    for c, (mean, scale) in zip((128 * i, HALF + 128 * i), both)
                )
                rows, lanes = slice(HH * ch, HH * ch + HH), slice(128 * i, 128 * i + 128)
                nh[0, rows, lanes], nl[0, rows, lanes] = split(x + x_two)
                nh[1, rows, lanes], nl[1, rows, lanes] = split(x - x_two)

        for j in range(2):
            y = dot3((wd[0, j], wd[1, j]), (nh[j], nl[j]), NT)
            for b in range(NBL):
                fwd[t, b, 8 * j : 8 * j + 8] = y[:, 128 * b : 128 * b + 128].reshape(8, 2 * KC, 128)

        send_slab(t, 0)
    leave(4)
    leave(6)
    send_slab(0, 1)
    send_slab(1, 1)
    load_there.wait()
    load_here.wait()

    special = (iota((KC, H), 0) == 0) & (me_s == 0)
    keep = jnp.where(special, 0.0, 1.0)

    def send_rows(b, t):
        channel = 8 + 2 * b + t
        send_all(channel, "space", lambda p: (inv.at[b, t, p], back.at[b, t, me_s]))
        flight[channel] = inv.at[b, t, pl.ds(0, NS - 1)]
        back[b, t, me_s] = inv[b, t, me_s]

    def spectral(b, between=None):
        for t in range(2):
            arrive(got.at[t, b, pl.ds(0, NS - 1)], 4 + 2 * t + b)

        for t in range(2):
            near = swap_eighths([got[t, b, a] for a in range(8)])
            far = swap_eighths([got[t, b, 8 + a] for a in range(8)])
            for ch in range(BS):
                rows, lanes = slice(2 * KC * ch, 2 * KC * ch + 2 * KC), slice(128 * t, 128 * t + 128)
                xh[0, rows, lanes], xl[0, rows, lanes] = split(near[ch] + far[ch])
                xh[1, rows, lanes], xl[1, rows, lanes] = split(near[ch] - far[ch])

        both = []
        for n in range(2):
            x = dot3((xh[n], xl[n]), (ht[0, n], ht[1, n]))
            both.append((x[:, :HALF], x[:, HALF:]))
        xc, xs = (jnp.concatenate(pair, axis=1).reshape(BS, 2, KC, H) for pair in zip(*both))
        y = jnp.stack([xc[:, 0] + keep * xs[:, 1], keep * xc[:, 1] - xs[:, 0]], axis=1).reshape(ROWS, H)
        first = jnp.maximum(dot3((m1h[b], m1l[b]), split(y)), 0.0)
        m2 = m2h[b], m2l[b]
        one = shrink(dot3(m2, split(first[:ROWS]))).reshape(BS, 2, KC, H)
        two = shrink(dot3(m2, split(first[ROWS:]))).reshape(BS, 2, KC, H)
        real = one[:, 0] + two[:, 0]
        imag = one[:, 1] - two[:, 1]
        channel = iota((BS, H), 0)
        extra_real, extra_imag = jnp.zeros((BS, H), F32), jnp.zeros((BS, H), F32)
        for ch in range(BS):
            extra_real = jnp.where(channel == ch, xc[ch, 1, 0:1], extra_real)
            extra_imag = jnp.where(channel == ch, -xs[ch, 1, 0:1], extra_imag)
        extra = jnp.concatenate([extra_real, extra_imag], axis=0)
        first = jnp.maximum(dot3((x1h[b, :, : 2 * BS], x1l[b, :, : 2 * BS]), split(extra)), 0.0)
        x2 = x2h[b, :, : 2 * BS], x2l[b, :, : 2 * BS]
        one = shrink(dot3(x2, split(first[: 2 * BS])))
        two = shrink(dot3(x2, split(first[2 * BS :])))
        extra_real = one[:BS] + two[:BS]
        extra_imag = one[BS:] - two[BS:]
        for ch in range(BS):
            z_real = jnp.where(special, 0.5 * (real[ch] - extra_imag[ch : ch + 1]), real[ch])
            z_imag = jnp.where(special, 0.5 * (imag[ch] + extra_real[ch : ch + 1]), imag[ch])
            for i, z in enumerate((z_real, z_imag)):
                rows = slice((2 * ch + i) * KC, (2 * ch + i + 1) * KC)
                for n in range(2):
                    zh[n, rows], zl[n, rows] = split(z[:, HALF * n : HALF * n + HALF])

        if between is not None:
            between()
        for t in range(2):
            sums = []
            for n in range(2):
                z = dot3((zh[n], zl[n]), (hb[0, n, t], hb[1, n, t]))
                zc = z[:, :128].reshape(BS, 2, KC, 128)
                zs = z[:, 128:].reshape(BS, 2, KC, 128)
                sums.append(jnp.stack([zc[:, 0] - zs[:, 1], zc[:, 1] + zs[:, 0]], axis=1).reshape(BS, 2 * KC, 128))
            near = swap_eighths([sums[0][ch] + sums[1][ch] for ch in range(BS)])
            far = swap_eighths([sums[0][ch] - sums[1][ch] for ch in range(BS)])
            for a in range(8):
                inv[b, t, a] = near[a]
                inv[b, t, 8 + a] = far[a]
            if t == 0:
                send_rows(b, t)

    def residual(b, t):
        channels = slice(BS * b, BS * b + BS)
        arrive(back.at[b, t, pl.ds(0, NS - 1)], 8 + 2 * b + t)
        sums = []
        for j in range(2):
            columns = split(back[b, t, 8 * j : 8 * j + 8].reshape(HALF, 128).T)
            sums.append(dot3(columns, (wd[0, j], wd[1, j])))
        rows = slice(HH * t, HH * t + HH)
        mixed[channels, rows, :HALF] = f[channels, rows, :HALF] + (sums[0] + sums[1]).reshape(BS, HH, HALF)
        mixed[channels, rows, HALF:] = f[channels, rows, HALF:] + (sums[0] - sums[1]).reshape(BS, HH, HALF)

        def pair(p):
            rows, lanes = cell_block(p, t)
            return mixed.at[pl.ds(BS * b, BS), rows, lanes], cells.at[t, me_c, pl.ds(BS * b, BS)]

        channel = 12 + 2 * b + t
        send_all(channel, "chan", pair)
        flight[channel] = cells.at[t, pl.ds(0, NC - 1), pl.ds(BS * b, BS)]
        rows, lanes = cell_block(me_c, t)
        cells[t, me_c, channels] = mixed[channels, rows, lanes]

    own = []

    def channel_mlp(t):
        for b in range(NBL):
            arrive(cells.at[t, pl.ds(0, NC - 1), pl.ds(BS * b, BS)], 12 + 2 * b + t)
        x = cells[t].reshape(C, 8, 128)
        mean = jnp.sum(x, axis=0) * (1.0 / C)
        d = x - mean
        scale = lax.rsqrt(jnp.sum(d * d, axis=0) * (1.0 / C) + 1e-05)
        n2[...] = (d * scale).reshape(C * 8, 128)
        x = jnp.concatenate([n2[pl.ds(i, C, stride=8), :] for i in range(8)], axis=1)
        v = gelu(dot3((w1h[...], w1l[...]), split(x)))
        y = dot3((w2h[...], w2l[...]), split(v))
        for i in range(8):
            ob[pl.ds(i, C, stride=8), :] = y[:, 128 * i : 128 * i + 128]
        ps[t] = cells[t] + ob[...].reshape(NC, CL, 8, 128)

        rows, lanes = cell_block(me_c, t)
        place = out.at[:, rows, lanes]
        send_all(16 + t, "chan", lambda p: (ps.at[t, p], place))
        flight[16 + t] = ps.at[t, pl.ds(0, NC - 1)]
        own.append(pltpu.make_async_copy(ps.at[t, me_c], place, load_sem.at[7 + t]))
        own[t].start()

    spectral(0)
    leave(8)
    send_rows(0, 1)
    spectral(1, lambda: residual(0, 0))
    residual(0, 1)
    leave(10)
    send_rows(1, 1)
    residual(1, 0)
    residual(1, 1)
    for t in range(2):
        channel_mlp(t)
    for t in range(2):
        own[t].wait()
        arrive(ps.at[t, pl.ds(0, NC - 1)], 16 + t)
    for channel in sorted(flight):
        leave(channel)


def local(field, gain_one, spec_one, spec_two, gain_two, mlp_in, mlp_out):
    vmem = pl.BlockSpec(memory_space=pltpu.VMEM)
    smem = pl.BlockSpec(memory_space=pltpu.SMEM)
    hbm = pl.BlockSpec(memory_space=pl.ANY)
    tables = [jnp.asarray(table) for table in (width_table(), *height_table())]
    scratch = [
        ((CL, HL, H), F32),
        ((2, 2, HALF, HALF), BF16),
        ((2, 2, HALF, H), BF16),
        ((2, 2, 2, HALF, HALF), BF16),
        ((HID, C), F32),
        ((C, HID), F32),
        ((HID, C), BF16),
        ((HID, C), BF16),
        ((C, HID), BF16),
        ((C, HID), BF16),
        ((2 * NBL, 4 * BS, ROWS), F32),
        ((NBL, 2 * ROWS, ROWS), BF16),
        ((NBL, 2 * ROWS, ROWS), BF16),
        ((NBL, ROWS, ROWS), BF16),
        ((NBL, ROWS, ROWS), BF16),
        ((NBL, 4 * BS, 128), BF16),
        ((NBL, 4 * BS, 128), BF16),
        ((NBL, 2 * BS, 128), BF16),
        ((NBL, 2 * BS, 128), BF16),
        ((2, NC, 2, 8, 128), F32),
        ((2, NC, 2, 8, 128), F32),
        ((2, NC, 2, 8, 128), F32),
        ((2, CL * HH, HALF), BF16),
        ((2, CL * HH, HALF), BF16),
        ((2, 2, NS, 2 * KC, 128), F32),
        ((2, 2, NS, 2 * KC, 128), F32),
        ((2, ROWS, HALF), BF16),
        ((2, ROWS, HALF), BF16),
        ((2, ROWS, HALF), BF16),
        ((2, ROWS, HALF), BF16),
        ((2, 2, NS, 2 * KC, 128), F32),
        ((2, 2, NS, 2 * KC, 128), F32),
        ((CL, HL, H), F32),
        ((2, NC, CL, 8, 128), F32),
        ((C * 8, 128), F32),
        ((C * 8, 128), F32),
        ((2, NC, CL, 8, 128), F32),
    ]
    return pl.pallas_call(
        kernel,
        out_shape=pltpu.VMEM((CL, HL, H), F32),
        in_specs=[smem, vmem, vmem, vmem] + [hbm] * 6,
        out_specs=pl.BlockSpec(memory_space=pltpu.VMEM),
        scratch_shapes=[pltpu.VMEM(shape, dtype) for shape, dtype in scratch]
        + [pltpu.SemaphoreType.DMA((9,)), pltpu.SemaphoreType.DMA((18,)), pltpu.SemaphoreType.DMA((18,))],
        compiler_params=pltpu.CompilerParams(
            collective_id=0, has_side_effects=True, vmem_limit_bytes=56 * 1024 * 1024
        ),
        name="afno_block",
    )(gain_one, spec_one, spec_two, gain_two.reshape(1, C), field, mlp_in, mlp_out, *tables)


def solution(mesh):
    placed = (
        P("chan", "space", None),
        P("chan"),
        P(None, "chan", None, None),
        P(None, "chan", None, None),
        P(),
        P(),
        P(),
    )
    return jax.shard_map(
        local, mesh=mesh, in_specs=placed, out_specs=P("chan", "space", None), check_vma=False
    )
```

```python
import functools

import jax
import jax.numpy as jnp
import ml_dtypes
import numpy as np
from jax import lax
from jax.experimental import pallas as pl
from jax.experimental.pallas import tpu as pltpu
from jax.sharding import PartitionSpec as P

MESH = pl.DeviceIdType.MESH
F32 = jnp.float32
BF16 = jnp.bfloat16

H = 512
C = 128
HID = 512
NS = 16
NC = 8
CL = C // NC
HL = H // NS
BS = 8
NBL = CL // BS
KC = 16
ROWS = BS * 2 * KC
HALF = H // 2
HH = HL // 2

NN = ((1,), (0,))
NT = ((1,), (1,))


def halves(table):
    high = table.astype(ml_dtypes.bfloat16)
    low = (table - high.astype(np.float64)).astype(ml_dtypes.bfloat16)
    return np.stack([high, low])


def width_table():
    row = np.arange(HALF)
    number = (row // (2 * KC)) * KC + row % KC
    imag = (row // KC) % 2 == 1
    both = []
    for odd in (0, 1):
        nyquist = imag & (number == 0) & (odd == 0)
        freq = np.where(nyquist, H // 2, 2 * number + odd)
        angle = 2 * np.pi / H * (freq[:, None] * np.arange(HALF)[None, :] % H)
        both.append(np.where((imag & ~nyquist)[:, None], -np.sin(angle), np.cos(angle)) / np.sqrt(H))
    return halves(np.stack(both))


def height_table():
    index = np.arange(HALF)
    h = index % 128 // HH * HL + index // 128 * HH + index % HH
    there, back = [], []
    for odd in (0, 1):
        angle = 2 * np.pi / H * (h[:, None] * (2 * index + odd)[None, :] % H)
        cosine, sine = np.cos(angle) / np.sqrt(H), np.sin(angle) / np.sqrt(H)
        there.append(np.concatenate([cosine, sine], axis=1))
        back.append(np.stack([np.concatenate([cosine.T[:, k], sine.T[:, k]], axis=1) for k in np.split(index, 2)]))
    return halves(np.stack(there)), halves(np.stack(back))


def split(x):
    high = x.astype(BF16)
    return high, (x - high.astype(F32)).astype(BF16)


def dot(a, b, dims=NN):
    return lax.dot_general(a, b, (dims, ((), ())), preferred_element_type=F32)


def dot3(a, b, dims=NN):
    left = jnp.concatenate([a[0], a[0], a[1]], axis=dims[0][0])
    right = jnp.concatenate([b[0], b[1], b[0]], axis=dims[1][0])
    return dot(left, right, dims)


def exact_dot(a, b, dims=NN):
    return lax.dot_general(a, b, (dims, ((), ())), precision=lax.Precision.HIGHEST, preferred_element_type=F32)


def iota(shape, axis):
    return lax.broadcasted_iota(jnp.int32, shape, axis)


def gelu(v):
    return 0.5 * v * (1.0 + lax.erf(v * 2.0**-0.5))


def shrink(v):
    return jnp.maximum(v - 0.01, 0.0) + jnp.minimum(v + 0.01, 0.0)


def swap_eighths(tiles):
    tiles = list(tiles)
    lane = iota(tiles[0].shape, 1)
    for step in (4, 2, 1):
        width = 16 * step
        low = lane // width % 2 == 0
        for i in range(8):
            if i & step == 0:
                one, two = tiles[i], tiles[i + step]
                tiles[i] = jnp.where(low, one, pltpu.roll(two, width, 1))
                tiles[i + step] = jnp.where(low, pltpu.roll(one, 128 - width, 1), two)
    return tiles


def kernel(
    gain_one_in, spec_one_in, spec_two_in, gain_two_in, field, mlp_in, mlp_out, width, there, here, out,
    gain_one, spec_one, spec_two, gain_two, f, wd, ht, hb, w1f, w2f, w1h, w1l, w2h, w2l, rw, m1h, m1l, m2h, m2l, x1h, x1l, x2h, x2l,
    part, parts, moments, nh, nl, fwd, got, xh, xl, zh, zl, inv, back, mixed, cells, n2, ob, ps,
    load_sem, send_sem, recv_sem,
):
    me_s = lax.axis_index("space")
    me_c = lax.axis_index("chan")

    loads = [(field.at[:, pl.ds(16 * i, 16)], f.at[:, pl.ds(16 * i, 16)]) for i in range(2)]
    loads += [(spec_one_in, spec_one), (spec_two_in, spec_two), (gain_one_in, gain_one), (gain_two_in, gain_two)]
    loads += [(width, wd), (there, ht), (here, hb), (mlp_in, w1f), (mlp_out, w2f)]
    loads = [pltpu.make_async_copy(src, dst, load_sem.at[i]) for i, (src, dst) in enumerate(loads)]
    for load in loads[:2]:
        load.start()
    load_width, load_there, load_here, load_in, load_out = loads[6:]

    barrier = pltpu.get_barrier_semaphore()

    def greet(axis, me, size):
        def one(i, carry):
            pl.semaphore_signal(barrier, inc=1, device_id={axis: lax.rem(me + i, size)}, device_id_type=MESH)
            return carry

        lax.fori_loop(1, size, one, 0)

    greet("chan", me_c, NC)
    greet("space", me_s, NS)

    def cell_block(p, t):
        return (
            pl.ds(pl.multiple_of(t * HH + p // 4 * 8, 8), 8),
            pl.ds(pl.multiple_of(lax.rem(p, 4) * 128, 128), 128),
        )

    flight = {}

    def arrive(ref, channel):
        pltpu.make_async_copy(ref, ref, recv_sem.at[channel]).wait()

    def leave(channel):
        ref = flight.pop(channel)
        pltpu.make_async_copy(ref, ref, send_sem.at[channel]).wait()

    def send_all(channel, axis, pair):
        me, size = (me_c, NC) if axis == "chan" else (me_s, NS)

        def one(i, carry):
            if axis == "chan":
                p = lax.rem(me // 2 + i // 2 + 2, 4) * 2 + lax.rem(me + i, 2)
            else:
                p = lax.rem(me // 4 + i // 4 + 2, 4) * 4 + lax.rem(me + i + 2, 4)
            src, dst = pair(p)
            pltpu.make_async_remote_copy(
                src_ref=src,
                dst_ref=dst,
                send_sem=send_sem.at[channel],
                recv_sem=recv_sem.at[channel],
                device_id={axis: p},
                device_id_type=MESH,
            ).start()
            return carry

        own = 4 if axis == "chan" else 10
        lax.fori_loop(0, own, one, 0)
        lax.fori_loop(own + 1, size, one, 0)

    for t in range(2):
        loads[t].wait()

        for p in range(NC):
            r, c = HH * t + 8 * (p // 4), 128 * (p % 4)
            x = f[:, r : r + 8, c : c + 128]
            total = jnp.sum(x, axis=0)
            d = x - total * (1.0 / CL)
            part[p, t, 0] = total
            part[p, t, 1] = jnp.sum(d * d, axis=0)
    for load in loads[2:]:
        load.start()
    pl.semaphore_wait(barrier, NC + NS - 2)
    send_all(0, "chan", lambda p: (part.at[p], parts.at[me_c]))
    flight[0] = part.at[pl.ds(0, NC - 1)]
    parts[me_c] = part[me_c]

    for load in loads[2:6]:
        load.wait()
    lift = jnp.concatenate(
        [
            iota((4 * BS, BS), 0) // 2 % BS == iota((4 * BS, BS), 1),
            iota((4 * BS, BS), 0) % BS == iota((4 * BS, BS), 1),
        ],
        axis=0,
    ).astype(F32)
    weights = jnp.concatenate([spec_one[...].reshape(4 * BS, BS), spec_two[...].reshape(4 * BS, BS)], axis=0)
    lifted = exact_dot(lift, weights, NT)
    high = lifted.astype(BF16)
    rest = lifted - high.astype(F32)
    middle_term = rest.astype(BF16)
    low = (rest - middle_term.astype(F32)).astype(BF16)
    wide = (iota((8 * BS, 8 * ROWS), 1) // (2 * KC) == iota((8 * BS, 8 * ROWS), 0)).astype(BF16)
    lane = iota((8 * BS, 8 * 128), 1)
    slim = ((lane // 128 * BS + lane % BS == iota((8 * BS, 8 * 128), 0)) & (lane % 128 < 2 * BS)).astype(BF16)

    def spread(rows, table):
        terms = jnp.concatenate([high[rows], middle_term[rows], low[rows]], axis=0)
        terms = dot(terms, table)
        return terms[: 4 * BS] + (terms[4 * BS : 8 * BS] + terms[8 * BS :])

    def complex_form(values, width, part_out, part_in, layer, b):
        variant = iota((4 * BS, width), 0) // (2 * BS)
        real = values[:, (4 * layer + b) * width : (4 * layer + b + 1) * width]
        imag = values[:, (4 * layer + 2 + b) * width : (4 * layer + 2 + b + 1) * width]
        real = jnp.where((variant == 1) & (part_out == 1), -real, real)
        imag = jnp.where((variant == 0) & (part_out == 0), -imag, imag)
        return jnp.where(part_out == part_in, real, imag)

    big = spread(slice(0, 4 * BS), wide)
    small = spread(slice(4 * BS, 8 * BS), slim)
    same_column = iota((KC, ROWS), 1) % KC == iota((KC, ROWS), 0)
    for b in range(NBL):
        for layer in range(2):
            part_out, part_in = iota((4 * BS, ROWS), 0) % 2, iota((4 * BS, ROWS), 1) // KC % 2
            rw[2 * b + layer] = complex_form(big, ROWS, part_out, part_in, layer, b)
            for r in range(4 * BS if layer == 0 else 2 * BS):
                row_high, row_low = split(jnp.where(same_column, rw[2 * b + layer, r : r + 1, :], 0.0))
                to_high, to_low = ((m1h, m1l), (m2h, m2l))[layer]
                to_high[b, KC * r : KC * r + KC] = row_high
                to_low[b, KC * r : KC * r + KC] = row_low
            part_out, part_in = iota((4 * BS, 128), 0) // BS % 2, iota((4 * BS, 128), 1) // BS % 2
            form = complex_form(small, 128, part_out, part_in, layer, b)
            if layer == 0:
                x1h[b], x1l[b] = split(form)
            else:
                x2h[b], x2l[b] = split(form[: 2 * BS])

    arrive(parts.at[pl.ds(0, NC - 1)], 0)
    totals = parts[:, :, 0]
    mean = jnp.sum(totals, axis=0) * (1.0 / C)
    apart = totals * (1.0 / CL) - mean
    var = (jnp.sum(parts[:, :, 1], axis=0) + CL * jnp.sum(apart * apart, axis=0)) * (1.0 / C)
    moments[me_c, :, 0] = mean
    moments[me_c, :, 1] = lax.rsqrt(var + 1e-05)
    send_all(2, "chan", lambda p: (moments.at[me_c], moments.at[me_c]))
    flight[2] = moments.at[pl.ds(0, NC - 1)]

    load_in.wait()
    load_out.wait()
    w1h[...], w1l[...] = split(w1f[...] * gain_two[...])
    w2h[...], w2l[...] = split(w2f[...])
    load_width.wait()

    arrive(moments.at[pl.ds(0, NC - 1)], 2)
    for b in range(NBL):
        for t in range(2):
            for i in range(2):
                both = []
                for k in (i, i + 2):
                    both.append([jnp.concatenate([moments[k, t, m], moments[k + 4, t, m]], axis=0) for m in range(2)])
                for ch in range(BS):
                    x, x_two = (
                        (f[BS * b + ch, HH * t : HH * t + HH, c : c + 128] - mean) * scale * gain_one[BS * b + ch]
                        for c, (mean, scale) in zip((128 * i, HALF + 128 * i), both)
                    )
                    row = (BS * t + ch) * HH
                    rows, lanes = slice(row, row + HH), slice(128 * i, 128 * i + 128)
                    nh[0, rows, lanes], nl[0, rows, lanes] = split(x + x_two)
                    nh[1, rows, lanes], nl[1, rows, lanes] = split(x - x_two)

        for j in range(2):
            y = dot3((wd[0, j], wd[1, j]), (nh[j], nl[j]), NT)
            for t in range(2):
                fwd[b, 8 * j : 8 * j + 8, t] = y[:, 128 * t : 128 * t + 128].reshape(8, 2 * KC, 128)

        if b == 1:
            leave(4)
        send_all(4 + b, "space", lambda p: (fwd.at[b, p], got.at[b, me_s]))
        flight[4 + b] = fwd.at[b, pl.ds(0, NS - 1)]
        got[b, me_s] = fwd[b, me_s]
    load_there.wait()
    load_here.wait()

    special = (iota((KC, H), 0) == 0) & (me_s == 0)
    keep = jnp.where(special, 0.0, 1.0)

    def send_rows(b, t):
        channel = 8 + 2 * b + t
        send_all(channel, "space", lambda p: (inv.at[b, t, p], back.at[b, t, me_s]))
        flight[channel] = inv.at[b, t, pl.ds(0, NS - 1)]
        back[b, t, me_s] = inv[b, t, me_s]

    def spectral(b, between=None):
        arrive(got.at[b, pl.ds(0, NS - 1)], 4 + b)
        for t in range(2):
            near = swap_eighths([got[b, a, t] for a in range(8)])
            far = swap_eighths([got[b, 8 + a, t] for a in range(8)])
            for ch in range(BS):
                rows, lanes = slice(2 * KC * ch, 2 * KC * ch + 2 * KC), slice(128 * t, 128 * t + 128)
                xh[0, rows, lanes], xl[0, rows, lanes] = split(near[ch] + far[ch])
                xh[1, rows, lanes], xl[1, rows, lanes] = split(near[ch] - far[ch])

        both = []
        for n in range(2):
            x = dot3((xh[n], xl[n]), (ht[0, n], ht[1, n]))
            both.append((x[:, :HALF], x[:, HALF:]))
        xc, xs = (jnp.concatenate(pair, axis=1).reshape(BS, 2, KC, H) for pair in zip(*both))
        y = jnp.stack([xc[:, 0] + keep * xs[:, 1], keep * xc[:, 1] - xs[:, 0]], axis=1).reshape(ROWS, H)
        first = jnp.maximum(dot3((m1h[b], m1l[b]), split(y)), 0.0)
        m2 = m2h[b], m2l[b]
        one = shrink(dot3(m2, split(first[:ROWS]))).reshape(BS, 2, KC, H)
        two = shrink(dot3(m2, split(first[ROWS:]))).reshape(BS, 2, KC, H)
        real = one[:, 0] + two[:, 0]
        imag = one[:, 1] - two[:, 1]
        channel = iota((BS, H), 0)
        extra_real, extra_imag = jnp.zeros((BS, H), F32), jnp.zeros((BS, H), F32)
        for ch in range(BS):
            extra_real = jnp.where(channel == ch, xc[ch, 1, 0:1], extra_real)
            extra_imag = jnp.where(channel == ch, -xs[ch, 1, 0:1], extra_imag)
        extra = jnp.concatenate([extra_real, extra_imag], axis=0)
        first = jnp.maximum(dot3((x1h[b, :, : 2 * BS], x1l[b, :, : 2 * BS]), split(extra)), 0.0)
        x2 = x2h[b, :, : 2 * BS], x2l[b, :, : 2 * BS]
        one = shrink(dot3(x2, split(first[: 2 * BS])))
        two = shrink(dot3(x2, split(first[2 * BS :])))
        extra_real = one[:BS] + two[:BS]
        extra_imag = one[BS:] - two[BS:]
        for ch in range(BS):
            z_real = jnp.where(special, 0.5 * (real[ch] - extra_imag[ch : ch + 1]), real[ch])
            z_imag = jnp.where(special, 0.5 * (imag[ch] + extra_real[ch : ch + 1]), imag[ch])
            for i, z in enumerate((z_real, z_imag)):
                rows = slice((2 * ch + i) * KC, (2 * ch + i + 1) * KC)
                for n in range(2):
                    zh[n, rows], zl[n, rows] = split(z[:, HALF * n : HALF * n + HALF])

        if between is not None:
            between()
        for t in range(2):
            sums = []
            for n in range(2):
                z = dot3((zh[n], zl[n]), (hb[0, n, t], hb[1, n, t]))
                zc = z[:, :128].reshape(BS, 2, KC, 128)
                zs = z[:, 128:].reshape(BS, 2, KC, 128)
                sums.append(jnp.stack([zc[:, 0] - zs[:, 1], zc[:, 1] + zs[:, 0]], axis=1).reshape(BS, 2 * KC, 128))
            near = swap_eighths([sums[0][ch] + sums[1][ch] for ch in range(BS)])
            far = swap_eighths([sums[0][ch] - sums[1][ch] for ch in range(BS)])
            for a in range(8):
                inv[b, t, a] = near[a]
                inv[b, t, 8 + a] = far[a]
            if t == 0:
                send_rows(b, t)

    def residual(b, t):
        channels = slice(BS * b, BS * b + BS)
        arrive(back.at[b, t, pl.ds(0, NS - 1)], 8 + 2 * b + t)
        sums = []
        for j in range(2):
            columns = split(back[b, t, 8 * j : 8 * j + 8].reshape(HALF, 128).T)
            sums.append(dot3(columns, (wd[0, j], wd[1, j])))
        rows = slice(HH * t, HH * t + HH)
        mixed[channels, rows, :HALF] = f[channels, rows, :HALF] + (sums[0] + sums[1]).reshape(BS, HH, HALF)
        mixed[channels, rows, HALF:] = f[channels, rows, HALF:] + (sums[0] - sums[1]).reshape(BS, HH, HALF)

        def pair(p):
            rows, lanes = cell_block(p, t)
            return mixed.at[pl.ds(BS * b, BS), rows, lanes], cells.at[t, me_c, pl.ds(BS * b, BS)]

        channel = 12 + 2 * b + t
        send_all(channel, "chan", pair)
        flight[channel] = cells.at[t, pl.ds(0, NC - 1), pl.ds(BS * b, BS)]
        rows, lanes = cell_block(me_c, t)
        cells[t, me_c, channels] = mixed[channels, rows, lanes]

    own = []

    def channel_mlp(t):
        for b in range(NBL):
            arrive(cells.at[t, pl.ds(0, NC - 1), pl.ds(BS * b, BS)], 12 + 2 * b + t)
        x = cells[t].reshape(C, 8, 128)
        mean = jnp.sum(x, axis=0) * (1.0 / C)
        d = x - mean
        scale = lax.rsqrt(jnp.sum(d * d, axis=0) * (1.0 / C) + 1e-05)
        n2[...] = (d * scale).reshape(C * 8, 128)
        x = jnp.concatenate([n2[pl.ds(i, C, stride=8), :] for i in range(8)], axis=1)
        v = gelu(dot3((w1h[...], w1l[...]), split(x)))
        y = dot3((w2h[...], w2l[...]), split(v))
        for i in range(8):
            ob[pl.ds(i, C, stride=8), :] = y[:, 128 * i : 128 * i + 128]
        ps[t] = cells[t] + ob[...].reshape(NC, CL, 8, 128)

        rows, lanes = cell_block(me_c, t)
        place = out.at[:, rows, lanes]
        send_all(16 + t, "chan", lambda p: (ps.at[t, p], place))
        flight[16 + t] = ps.at[t, pl.ds(0, NC - 1)]
        own.append(pltpu.make_async_copy(ps.at[t, me_c], place, load_sem.at[11 + t]))
        own[t].start()

    spectral(0)
    send_rows(0, 1)
    spectral(1)
    residual(0, 0)
    residual(0, 1)
    leave(10)
    send_rows(1, 1)
    residual(1, 0)
    residual(1, 1)
    for t in range(2):
        channel_mlp(t)
    for t in range(2):
        own[t].wait()
        arrive(ps.at[t, pl.ds(0, NC - 1)], 16 + t)
    for channel in sorted(flight):
        leave(channel)


def local(field, gain_one, spec_one, spec_two, gain_two, mlp_in, mlp_out):
    hbm = pl.BlockSpec(memory_space=pl.ANY)
    tables = [jnp.asarray(table) for table in (width_table(), *height_table())]
    scratch = [
        ((2, NBL, BS, BS), F32),
        ((2, NBL, BS, BS), F32),
        ((1, C), F32),
        ((CL, HL, H), F32),
        ((2, 2, HALF, HALF), BF16),
        ((2, 2, HALF, H), BF16),
        ((2, 2, 2, HALF, HALF), BF16),
        ((HID, C), F32),
        ((C, HID), F32),
        ((HID, C), BF16),
        ((HID, C), BF16),
        ((C, HID), BF16),
        ((C, HID), BF16),
        ((2 * NBL, 4 * BS, ROWS), F32),
        ((NBL, 2 * ROWS, ROWS), BF16),
        ((NBL, 2 * ROWS, ROWS), BF16),
        ((NBL, ROWS, ROWS), BF16),
        ((NBL, ROWS, ROWS), BF16),
        ((NBL, 4 * BS, 128), BF16),
        ((NBL, 4 * BS, 128), BF16),
        ((NBL, 2 * BS, 128), BF16),
        ((NBL, 2 * BS, 128), BF16),
        ((NC, 2, 2, 8, 128), F32),
        ((NC, 2, 2, 8, 128), F32),
        ((NC, 2, 2, 8, 128), F32),
        ((2, CL * HH, HALF), BF16),
        ((2, CL * HH, HALF), BF16),
        ((NBL, NS, 2, 2 * KC, 128), F32),
        ((NBL, NS, 2, 2 * KC, 128), F32),
        ((2, ROWS, HALF), BF16),
        ((2, ROWS, HALF), BF16),
        ((2, ROWS, HALF), BF16),
        ((2, ROWS, HALF), BF16),
        ((2, 2, NS, 2 * KC, 128), F32),
        ((2, 2, NS, 2 * KC, 128), F32),
        ((CL, HL, H), F32),
        ((2, NC, CL, 8, 128), F32),
        ((C * 8, 128), F32),
        ((C * 8, 128), F32),
        ((2, NC, CL, 8, 128), F32),
    ]
    return pl.pallas_call(
        kernel,
        out_shape=pltpu.VMEM((CL, HL, H), F32),
        in_specs=[hbm] * 10,
        out_specs=pl.BlockSpec(memory_space=pltpu.VMEM),
        scratch_shapes=[pltpu.SMEM((CL,), F32)]
        + [pltpu.VMEM(shape, dtype) for shape, dtype in scratch]
        + [pltpu.SemaphoreType.DMA((13,)), pltpu.SemaphoreType.DMA((18,)), pltpu.SemaphoreType.DMA((18,))],
        compiler_params=pltpu.CompilerParams(
            collective_id=0, has_side_effects=True, vmem_limit_bytes=56 * 1024 * 1024
        ),
        name="afno_block",
    )(gain_one, spec_one, spec_two, gain_two.reshape(1, C), field, mlp_in, mlp_out, *tables)


def solution(mesh):
    placed = (
        P("chan", "space", None),
        P("chan"),
        P(None, "chan", None, None),
        P(None, "chan", None, None),
        P(),
        P(),
        P(),
    )
    return jax.shard_map(
        local, mesh=mesh, in_specs=placed, out_specs=P("chan", "space", None), check_vma=False
    )
```

```python
import functools

import jax
import jax.numpy as jnp
import ml_dtypes
import numpy as np
from jax import lax
from jax.experimental import pallas as pl
from jax.experimental.pallas import tpu as pltpu
from jax.sharding import PartitionSpec as P

MESH = pl.DeviceIdType.MESH
F32 = jnp.float32
BF16 = jnp.bfloat16

H = 512
C = 128
HID = 512
NS = 16
NC = 8
CL = C // NC
HL = H // NS
BS = 8
NBL = CL // BS
KC = 16
ROWS = BS * 2 * KC
HALF = H // 2
HH = HL // 2

NN = ((1,), (0,))
NT = ((1,), (1,))


def halves(table):
    high = table.astype(ml_dtypes.bfloat16)
    low = (table - high.astype(np.float64)).astype(ml_dtypes.bfloat16)
    return np.stack([high, low])


def width_table():
    row = np.arange(HALF)
    number = (row // (2 * KC)) * KC + row % KC
    imag = (row // KC) % 2 == 1
    both = []
    for odd in (0, 1):
        nyquist = imag & (number == 0) & (odd == 0)
        freq = np.where(nyquist, H // 2, 2 * number + odd)
        angle = 2 * np.pi / H * (freq[:, None] * np.arange(HALF)[None, :] % H)
        both.append(np.where((imag & ~nyquist)[:, None], -np.sin(angle), np.cos(angle)) / np.sqrt(H))
    return halves(np.stack(both))


def height_table():
    index = np.arange(HALF)
    h = index % 128 // HH * HL + index // 128 * HH + index % HH
    there, back = [], []
    for odd in (0, 1):
        angle = 2 * np.pi / H * (h[:, None] * (2 * index + odd)[None, :] % H)
        cosine, sine = np.cos(angle) / np.sqrt(H), np.sin(angle) / np.sqrt(H)
        there.append(np.concatenate([cosine, sine], axis=1))
        back.append(np.stack([np.concatenate([cosine.T[:, k], sine.T[:, k]], axis=1) for k in np.split(index, 2)]))
    return halves(np.stack(there)), halves(np.stack(back))


def split(x):
    high = x.astype(BF16)
    return high, (x - high.astype(F32)).astype(BF16)


def dot(a, b, dims=NN):
    return lax.dot_general(a, b, (dims, ((), ())), preferred_element_type=F32)


def dot3(a, b, dims=NN):
    left = jnp.concatenate([a[0], a[0], a[1]], axis=dims[0][0])
    right = jnp.concatenate([b[0], b[1], b[0]], axis=dims[1][0])
    return dot(left, right, dims)


def exact_dot(a, b, dims=NN):
    return lax.dot_general(a, b, (dims, ((), ())), precision=lax.Precision.HIGHEST, preferred_element_type=F32)


def iota(shape, axis):
    return lax.broadcasted_iota(jnp.int32, shape, axis)


def gelu(v):
    return 0.5 * v * (1.0 + lax.erf(v * 2.0**-0.5))


def shrink(v):
    return jnp.maximum(v - 0.01, 0.0) + jnp.minimum(v + 0.01, 0.0)


def swap_eighths(tiles):
    tiles = list(tiles)
    lane = iota(tiles[0].shape, 1)
    for step in (4, 2, 1):
        width = 16 * step
        low = lane // width % 2 == 0
        for i in range(8):
            if i & step == 0:
                one, two = tiles[i], tiles[i + step]
                tiles[i] = jnp.where(low, one, pltpu.roll(two, width, 1))
                tiles[i + step] = jnp.where(low, pltpu.roll(one, 128 - width, 1), two)
    return tiles


def kernel(
    gain_one_in, spec_one_in, spec_two_in, gain_two_in, field, mlp_in, mlp_out, width, there, here, out,
    gain_one, spec_one, spec_two, gain_two, f, wd, ht, hb, w1f, w2f, w1h, w1l, w2h, w2l, rw, m1h, m1l, m2h, m2l, x1h, x1l, x2h, x2l,
    part, parts, moments, nh, nl, fwd, got, xh, xl, zh, zl, inv, back, mixed, cells, n2, ob, ps,
    load_sem, send_sem, recv_sem,
):
    me_s = lax.axis_index("space")
    me_c = lax.axis_index("chan")

    loads = [(field.at[:, pl.ds(16 * i, 16)], f.at[:, pl.ds(16 * i, 16)]) for i in range(2)]
    loads += [(spec_one_in, spec_one), (spec_two_in, spec_two), (gain_one_in, gain_one), (gain_two_in, gain_two)]
    loads += [(width, wd), (there, ht), (here, hb), (mlp_in, w1f), (mlp_out, w2f)]
    loads = [pltpu.make_async_copy(src, dst, load_sem.at[i]) for i, (src, dst) in enumerate(loads)]
    for load in loads[:2]:
        load.start()
    load_width, load_there, load_here, load_in, load_out = loads[6:]

    barrier = pltpu.get_barrier_semaphore()

    def greet(axis, me, size):
        def one(i, carry):
            pl.semaphore_signal(barrier, inc=1, device_id={axis: lax.rem(me + i, size)}, device_id_type=MESH)
            return carry

        lax.fori_loop(1, size, one, 0)

    greet("chan", me_c, NC)
    greet("space", me_s, NS)

    def cell_block(p, t):
        return (
            pl.ds(pl.multiple_of(t * HH + p // 4 * 8, 8), 8),
            pl.ds(pl.multiple_of(lax.rem(p, 4) * 128, 128), 128),
        )

    flight = {}

    def arrive(ref, channel):
        pltpu.make_async_copy(ref, ref, recv_sem.at[channel]).wait()

    def leave(channel):
        ref = flight.pop(channel)
        pltpu.make_async_copy(ref, ref, send_sem.at[channel]).wait()

    def send_all(channel, axis, pair):
        me, size = (me_c, NC) if axis == "chan" else (me_s, NS)

        def one(i, carry):
            if axis == "chan":
                p = lax.rem(me // 2 + i // 2 + 2, 4) * 2 + lax.rem(me + i, 2)
            else:
                p = lax.rem(me // 4 + i // 4 + 2, 4) * 4 + lax.rem(me + i + 2, 4)
            src, dst = pair(p)
            pltpu.make_async_remote_copy(
                src_ref=src,
                dst_ref=dst,
                send_sem=send_sem.at[channel],
                recv_sem=recv_sem.at[channel],
                device_id={axis: p},
                device_id_type=MESH,
            ).start()
            return carry

        own = 4 if axis == "chan" else 10
        lax.fori_loop(0, own, one, 0)
        lax.fori_loop(own + 1, size, one, 0)

    for t in range(2):
        loads[t].wait()

        for p in range(NC):
            r, c = HH * t + 8 * (p // 4), 128 * (p % 4)
            x = f[:, r : r + 8, c : c + 128]
            total = jnp.sum(x, axis=0)
            d = x - total * (1.0 / CL)
            part[p, t, 0] = total
            part[p, t, 1] = jnp.sum(d * d, axis=0)
    for load in loads[2:]:
        load.start()
    pl.semaphore_wait(barrier, NC + NS - 2)
    send_all(0, "chan", lambda p: (part.at[p], parts.at[me_c]))
    flight[0] = part.at[pl.ds(0, NC - 1)]
    parts[me_c] = part[me_c]

    for load in loads[2:6]:
        load.wait()
    lift = jnp.concatenate(
        [
            iota((4 * BS, BS), 0) // 2 % BS == iota((4 * BS, BS), 1),
            iota((4 * BS, BS), 0) % BS == iota((4 * BS, BS), 1),
        ],
        axis=0,
    ).astype(F32)
    weights = jnp.concatenate([spec_one[...].reshape(4 * BS, BS), spec_two[...].reshape(4 * BS, BS)], axis=0)
    lifted = exact_dot(lift, weights, NT)
    high = lifted.astype(BF16)
    rest = lifted - high.astype(F32)
    middle_term = rest.astype(BF16)
    low = (rest - middle_term.astype(F32)).astype(BF16)
    wide = (iota((8 * BS, 8 * ROWS), 1) // (2 * KC) == iota((8 * BS, 8 * ROWS), 0)).astype(BF16)
    lane = iota((8 * BS, 8 * 128), 1)
    slim = ((lane // 128 * BS + lane % BS == iota((8 * BS, 8 * 128), 0)) & (lane % 128 < 2 * BS)).astype(BF16)

    def spread(rows, table):
        terms = jnp.concatenate([high[rows], middle_term[rows], low[rows]], axis=0)
        terms = dot(terms, table)
        return terms[: 4 * BS] + (terms[4 * BS : 8 * BS] + terms[8 * BS :])

    def complex_form(values, width, part_out, part_in, layer, b):
        variant = iota((4 * BS, width), 0) // (2 * BS)
        real = values[:, (4 * layer + b) * width : (4 * layer + b + 1) * width]
        imag = values[:, (4 * layer + 2 + b) * width : (4 * layer + 2 + b + 1) * width]
        real = jnp.where((variant == 1) & (part_out == 1), -real, real)
        imag = jnp.where((variant == 0) & (part_out == 0), -imag, imag)
        return jnp.where(part_out == part_in, real, imag)

    big = spread(slice(0, 4 * BS), wide)
    small = spread(slice(4 * BS, 8 * BS), slim)
    same_column = iota((KC, ROWS), 1) % KC == iota((KC, ROWS), 0)
    for b in range(NBL):
        for layer in range(2):
            part_out, part_in = iota((4 * BS, ROWS), 0) % 2, iota((4 * BS, ROWS), 1) // KC % 2
            rw[2 * b + layer] = complex_form(big, ROWS, part_out, part_in, layer, b)
            for r in range(4 * BS if layer == 0 else 2 * BS):
                row_high, row_low = split(jnp.where(same_column, rw[2 * b + layer, r : r + 1, :], 0.0))
                to_high, to_low = ((m1h, m1l), (m2h, m2l))[layer]
                to_high[b, KC * r : KC * r + KC] = row_high
                to_low[b, KC * r : KC * r + KC] = row_low
            part_out, part_in = iota((4 * BS, 128), 0) // BS % 2, iota((4 * BS, 128), 1) // BS % 2
            form = complex_form(small, 128, part_out, part_in, layer, b)
            if layer == 0:
                x1h[b], x1l[b] = split(form)
            else:
                x2h[b], x2l[b] = split(form[: 2 * BS])

    arrive(parts.at[pl.ds(0, NC - 1)], 0)
    totals = parts[:, :, 0]
    mean = jnp.sum(totals, axis=0) * (1.0 / C)
    apart = totals * (1.0 / CL) - mean
    var = (jnp.sum(parts[:, :, 1], axis=0) + CL * jnp.sum(apart * apart, axis=0)) * (1.0 / C)
    moments[me_c, :, 0] = mean
    moments[me_c, :, 1] = lax.rsqrt(var + 1e-05)
    send_all(2, "chan", lambda p: (moments.at[me_c], moments.at[me_c]))
    flight[2] = moments.at[pl.ds(0, NC - 1)]

    load_in.wait()
    load_out.wait()
    w1h[...], w1l[...] = split(w1f[...] * gain_two[...])
    w2h[...], w2l[...] = split(w2f[...])
    load_width.wait()

    arrive(moments.at[pl.ds(0, NC - 1)], 2)
    for b in range(NBL):
        for t in range(2):
            for i in range(2):
                both = []
                for k in (i, i + 2):
                    both.append([jnp.concatenate([moments[k, t, m], moments[k + 4, t, m]], axis=0) for m in range(2)])
                for ch in range(BS):
                    x, x_two = (
                        (f[BS * b + ch, HH * t : HH * t + HH, c : c + 128] - mean) * scale * gain_one[BS * b + ch]
                        for c, (mean, scale) in zip((128 * i, HALF + 128 * i), both)
                    )
                    row = (BS * t + ch) * HH
                    rows, lanes = slice(row, row + HH), slice(128 * i, 128 * i + 128)
                    nh[0, rows, lanes], nl[0, rows, lanes] = split(x + x_two)
                    nh[1, rows, lanes], nl[1, rows, lanes] = split(x - x_two)

        for j in range(2):
            y = dot3((wd[0, j], wd[1, j]), (nh[j], nl[j]), NT)
            for t in range(2):
                fwd[b, 8 * j : 8 * j + 8, t] = y[:, 128 * t : 128 * t + 128].reshape(8, 2 * KC, 128)

        if b == 1:
            leave(4)
        send_all(4 + b, "space", lambda p: (fwd.at[b, p], got.at[b, me_s]))
        flight[4 + b] = fwd.at[b, pl.ds(0, NS - 1)]
        got[b, me_s] = fwd[b, me_s]
    load_there.wait()
    load_here.wait()

    special = (iota((KC, H), 0) == 0) & (me_s == 0)
    keep = jnp.where(special, 0.0, 1.0)

    def send_rows(b, t):
        channel = 8 + 2 * b + t
        send_all(channel, "space", lambda p: (inv.at[b, t, p], back.at[b, t, me_s]))
        flight[channel] = inv.at[b, t, pl.ds(0, NS - 1)]
        back[b, t, me_s] = inv[b, t, me_s]

    def spectral(b, between=None):
        arrive(got.at[b, pl.ds(0, NS - 1)], 4 + b)
        for t in range(2):
            near = swap_eighths([got[b, a, t] for a in range(8)])
            far = swap_eighths([got[b, 8 + a, t] for a in range(8)])
            for ch in range(BS):
                rows, lanes = slice(2 * KC * ch, 2 * KC * ch + 2 * KC), slice(128 * t, 128 * t + 128)
                xh[0, rows, lanes], xl[0, rows, lanes] = split(near[ch] + far[ch])
                xh[1, rows, lanes], xl[1, rows, lanes] = split(near[ch] - far[ch])

        both = []
        for n in range(2):
            x = dot3((xh[n], xl[n]), (ht[0, n], ht[1, n]))
            both.append((x[:, :HALF], x[:, HALF:]))
        xc, xs = (jnp.concatenate(pair, axis=1).reshape(BS, 2, KC, H) for pair in zip(*both))
        y = jnp.stack([xc[:, 0] + keep * xs[:, 1], keep * xc[:, 1] - xs[:, 0]], axis=1).reshape(ROWS, H)
        first = jnp.maximum(dot3((m1h[b], m1l[b]), split(y)), 0.0)
        m2 = m2h[b], m2l[b]
        one = shrink(dot3(m2, split(first[:ROWS]))).reshape(BS, 2, KC, H)
        two = shrink(dot3(m2, split(first[ROWS:]))).reshape(BS, 2, KC, H)
        real = one[:, 0] + two[:, 0]
        imag = one[:, 1] - two[:, 1]
        channel = iota((BS, H), 0)
        extra_real, extra_imag = jnp.zeros((BS, H), F32), jnp.zeros((BS, H), F32)
        for ch in range(BS):
            extra_real = jnp.where(channel == ch, xc[ch, 1, 0:1], extra_real)
            extra_imag = jnp.where(channel == ch, -xs[ch, 1, 0:1], extra_imag)
        extra = jnp.concatenate([extra_real, extra_imag], axis=0)
        first = jnp.maximum(dot3((x1h[b, :, : 2 * BS], x1l[b, :, : 2 * BS]), split(extra)), 0.0)
        x2 = x2h[b, :, : 2 * BS], x2l[b, :, : 2 * BS]
        one = shrink(dot3(x2, split(first[: 2 * BS])))
        two = shrink(dot3(x2, split(first[2 * BS :])))
        extra_real = one[:BS] + two[:BS]
        extra_imag = one[BS:] - two[BS:]
        for ch in range(BS):
            z_real = jnp.where(special, 0.5 * (real[ch] - extra_imag[ch : ch + 1]), real[ch])
            z_imag = jnp.where(special, 0.5 * (imag[ch] + extra_real[ch : ch + 1]), imag[ch])
            for i, z in enumerate((z_real, z_imag)):
                rows = slice((2 * ch + i) * KC, (2 * ch + i + 1) * KC)
                for n in range(2):
                    zh[n, rows], zl[n, rows] = split(z[:, HALF * n : HALF * n + HALF])

        for t in range(2):
            sums = []
            for n in range(2):
                z = dot3((zh[n], zl[n]), (hb[0, n, t], hb[1, n, t]))
                zc = z[:, :128].reshape(BS, 2, KC, 128)
                zs = z[:, 128:].reshape(BS, 2, KC, 128)
                sums.append(jnp.stack([zc[:, 0] - zs[:, 1], zc[:, 1] + zs[:, 0]], axis=1).reshape(BS, 2 * KC, 128))
            near = swap_eighths([sums[0][ch] + sums[1][ch] for ch in range(BS)])
            far = swap_eighths([sums[0][ch] - sums[1][ch] for ch in range(BS)])
            for a in range(8):
                inv[b, t, a] = near[a]
                inv[b, t, 8 + a] = far[a]
            if t == 0:
                send_rows(b, t)
                if between is not None:
                    between()

    def residual(b, t):
        channels = slice(BS * b, BS * b + BS)
        arrive(back.at[b, t, pl.ds(0, NS - 1)], 8 + 2 * b + t)
        sums = []
        for j in range(2):
            columns = split(back[b, t, 8 * j : 8 * j + 8].reshape(HALF, 128).T)
            sums.append(dot3(columns, (wd[0, j], wd[1, j])))
        rows = slice(HH * t, HH * t + HH)
        mixed[channels, rows, :HALF] = f[channels, rows, :HALF] + (sums[0] + sums[1]).reshape(BS, HH, HALF)
        mixed[channels, rows, HALF:] = f[channels, rows, HALF:] + (sums[0] - sums[1]).reshape(BS, HH, HALF)

        def pair(p):
            rows, lanes = cell_block(p, t)
            return mixed.at[pl.ds(BS * b, BS), rows, lanes], cells.at[t, me_c, pl.ds(BS * b, BS)]

        channel = 12 + 2 * b + t
        send_all(channel, "chan", pair)
        flight[channel] = cells.at[t, pl.ds(0, NC - 1), pl.ds(BS * b, BS)]
        rows, lanes = cell_block(me_c, t)
        cells[t, me_c, channels] = mixed[channels, rows, lanes]

    own = []

    def channel_mlp(t):
        for b in range(NBL):
            arrive(cells.at[t, pl.ds(0, NC - 1), pl.ds(BS * b, BS)], 12 + 2 * b + t)
        x = cells[t].reshape(C, 8, 128)
        mean = jnp.sum(x, axis=0) * (1.0 / C)
        d = x - mean
        scale = lax.rsqrt(jnp.sum(d * d, axis=0) * (1.0 / C) + 1e-05)
        n2[...] = (d * scale).reshape(C * 8, 128)
        x = jnp.concatenate([n2[pl.ds(i, C, stride=8), :] for i in range(8)], axis=1)
        v = gelu(dot3((w1h[...], w1l[...]), split(x)))
        y = dot3((w2h[...], w2l[...]), split(v))
        for i in range(8):
            ob[pl.ds(i, C, stride=8), :] = y[:, 128 * i : 128 * i + 128]
        ps[t] = cells[t] + ob[...].reshape(NC, CL, 8, 128)

        rows, lanes = cell_block(me_c, t)
        place = out.at[:, rows, lanes]
        send_all(16 + t, "chan", lambda p: (ps.at[t, p], place))
        flight[16 + t] = ps.at[t, pl.ds(0, NC - 1)]
        own.append(pltpu.make_async_copy(ps.at[t, me_c], place, load_sem.at[11 + t]))
        own[t].start()

    spectral(0)
    send_rows(0, 1)
    spectral(1, lambda: residual(0, 0))
    residual(0, 1)
    leave(10)
    send_rows(1, 1)
    residual(1, 0)
    residual(1, 1)
    for t in range(2):
        channel_mlp(t)
    for channel in sorted(flight):
        leave(channel)
    for t in range(2):
        own[t].wait()
        arrive(ps.at[t, pl.ds(0, NC - 1)], 16 + t)


def local(field, gain_one, spec_one, spec_two, gain_two, mlp_in, mlp_out):
    hbm = pl.BlockSpec(memory_space=pl.ANY)
    tables = [jnp.asarray(table) for table in (width_table(), *height_table())]
    scratch = [
        ((2, NBL, BS, BS), F32),
        ((2, NBL, BS, BS), F32),
        ((1, C), F32),
        ((CL, HL, H), F32),
        ((2, 2, HALF, HALF), BF16),
        ((2, 2, HALF, H), BF16),
        ((2, 2, 2, HALF, HALF), BF16),
        ((HID, C), F32),
        ((C, HID), F32),
        ((HID, C), BF16),
        ((HID, C), BF16),
        ((C, HID), BF16),
        ((C, HID), BF16),
        ((2 * NBL, 4 * BS, ROWS), F32),
        ((NBL, 2 * ROWS, ROWS), BF16),
        ((NBL, 2 * ROWS, ROWS), BF16),
        ((NBL, ROWS, ROWS), BF16),
        ((NBL, ROWS, ROWS), BF16),
        ((NBL, 4 * BS, 128), BF16),
        ((NBL, 4 * BS, 128), BF16),
        ((NBL, 2 * BS, 128), BF16),
        ((NBL, 2 * BS, 128), BF16),
        ((NC, 2, 2, 8, 128), F32),
        ((NC, 2, 2, 8, 128), F32),
        ((NC, 2, 2, 8, 128), F32),
        ((2, CL * HH, HALF), BF16),
        ((2, CL * HH, HALF), BF16),
        ((NBL, NS, 2, 2 * KC, 128), F32),
        ((NBL, NS, 2, 2 * KC, 128), F32),
        ((2, ROWS, HALF), BF16),
        ((2, ROWS, HALF), BF16),
        ((2, ROWS, HALF), BF16),
        ((2, ROWS, HALF), BF16),
        ((2, 2, NS, 2 * KC, 128), F32),
        ((2, 2, NS, 2 * KC, 128), F32),
        ((CL, HL, H), F32),
        ((2, NC, CL, 8, 128), F32),
        ((C * 8, 128), F32),
        ((C * 8, 128), F32),
        ((2, NC, CL, 8, 128), F32),
    ]
    return pl.pallas_call(
        kernel,
        out_shape=pltpu.VMEM((CL, HL, H), F32),
        in_specs=[hbm] * 10,
        out_specs=pl.BlockSpec(memory_space=pltpu.VMEM),
        scratch_shapes=[pltpu.SMEM((CL,), F32)]
        + [pltpu.VMEM(shape, dtype) for shape, dtype in scratch]
        + [pltpu.SemaphoreType.DMA((13,)), pltpu.SemaphoreType.DMA((18,)), pltpu.SemaphoreType.DMA((18,))],
        compiler_params=pltpu.CompilerParams(
            collective_id=0, has_side_effects=True, vmem_limit_bytes=56 * 1024 * 1024
        ),
        name="afno_block",
    )(gain_one, spec_one, spec_two, gain_two.reshape(1, C), field, mlp_in, mlp_out, *tables)


def solution(mesh):
    placed = (
        P("chan", "space", None),
        P("chan"),
        P(None, "chan", None, None),
        P(None, "chan", None, None),
        P(),
        P(),
        P(),
    )
    return jax.shard_map(
        local, mesh=mesh, in_specs=placed, out_specs=P("chan", "space", None), check_vma=False
    )
```

```python
import functools

import jax
import jax.numpy as jnp
import ml_dtypes
import numpy as np
from jax import lax
from jax.experimental import pallas as pl
from jax.experimental.pallas import tpu as pltpu
from jax.sharding import PartitionSpec as P

MESH = pl.DeviceIdType.MESH
F32 = jnp.float32
BF16 = jnp.bfloat16

H = 512
C = 128
HID = 512
NS = 16
NC = 8
CL = C // NC
HL = H // NS
BS = 8
NBL = CL // BS
KC = 16
ROWS = BS * 2 * KC
HALF = H // 2
HH = HL // 2

NN = ((1,), (0,))
NT = ((1,), (1,))


def halves(table):
    high = table.astype(ml_dtypes.bfloat16)
    low = (table - high.astype(np.float64)).astype(ml_dtypes.bfloat16)
    return np.stack([high, low])


def width_table():
    row = np.arange(HALF)
    number = (row // (2 * KC)) * KC + row % KC
    imag = (row // KC) % 2 == 1
    both = []
    for odd in (0, 1):
        nyquist = imag & (number == 0) & (odd == 0)
        freq = np.where(nyquist, H // 2, 2 * number + odd)
        angle = 2 * np.pi / H * (freq[:, None] * np.arange(HALF)[None, :] % H)
        both.append(np.where((imag & ~nyquist)[:, None], -np.sin(angle), np.cos(angle)) / np.sqrt(H))
    return halves(np.stack(both))


def height_table():
    index = np.arange(HALF)
    h = index % 128 // HH * HL + index // 128 * HH + index % HH
    there, back = [], []
    for odd in (0, 1):
        angle = 2 * np.pi / H * (h[:, None] * (2 * index + odd)[None, :] % H)
        cosine, sine = np.cos(angle) / np.sqrt(H), np.sin(angle) / np.sqrt(H)
        there.append(np.concatenate([cosine, sine], axis=1))
        back.append(np.stack([np.concatenate([cosine.T[:, k], sine.T[:, k]], axis=1) for k in np.split(index, 2)]))
    return halves(np.stack(there)), halves(np.stack(back))


def split(x):
    high = x.astype(BF16)
    return high, (x - high.astype(F32)).astype(BF16)


def dot(a, b, dims=NN):
    return lax.dot_general(a, b, (dims, ((), ())), preferred_element_type=F32)


def dot3(a, b, dims=NN):
    left = jnp.concatenate([a[0], a[0], a[1]], axis=dims[0][0])
    right = jnp.concatenate([b[0], b[1], b[0]], axis=dims[1][0])
    return dot(left, right, dims)


def exact_dot(a, b, dims=NN):
    return lax.dot_general(a, b, (dims, ((), ())), precision=lax.Precision.HIGHEST, preferred_element_type=F32)


def iota(shape, axis):
    return lax.broadcasted_iota(jnp.int32, shape, axis)


def gelu(v):
    return 0.5 * v * (1.0 + lax.erf(v * 2.0**-0.5))


def shrink(v):
    return jnp.maximum(v - 0.01, 0.0) + jnp.minimum(v + 0.01, 0.0)


def swap_eighths(tiles):
    tiles = list(tiles)
    lane = iota(tiles[0].shape, 1)
    for step in (4, 2, 1):
        width = 16 * step
        low = lane // width % 2 == 0
        for i in range(8):
            if i & step == 0:
                one, two = tiles[i], tiles[i + step]
                tiles[i] = jnp.where(low, one, pltpu.roll(two, width, 1))
                tiles[i + step] = jnp.where(low, pltpu.roll(one, 128 - width, 1), two)
    return tiles


def kernel(
    gain_one_in, spec_one_in, spec_two_in, gain_two_in, field, mlp_in, mlp_out, width, there, here, out,
    gain_one, spec_one, spec_two, gain_two, f, wd, ht, hb, w1f, w2f, w1h, w1l, w2h, w2l, rw, m1h, m1l, m2h, m2l, x1h, x1l, x2h, x2l,
    part, parts, moments, nh, nl, fwd, got, xh, xl, zh, zl, inv, back, mixed, cells, n2, ob, ps,
    load_sem, send_sem, recv_sem,
):
    me_s = lax.axis_index("space")
    me_c = lax.axis_index("chan")

    loads = [(field.at[:, pl.ds(16 * i, 16)], f.at[:, pl.ds(16 * i, 16)]) for i in range(2)]
    loads += [(spec_one_in, spec_one), (spec_two_in, spec_two), (gain_one_in, gain_one), (gain_two_in, gain_two)]
    loads += [(width, wd), (there, ht), (here, hb), (mlp_in, w1f), (mlp_out, w2f)]
    loads = [pltpu.make_async_copy(src, dst, load_sem.at[i]) for i, (src, dst) in enumerate(loads)]
    for load in loads[:2]:
        load.start()
    load_width, load_there, load_here, load_in, load_out = loads[6:]

    barrier = pltpu.get_barrier_semaphore()

    def greet(axis, me, size):
        def one(i, carry):
            pl.semaphore_signal(barrier, inc=1, device_id={axis: lax.rem(me + i, size)}, device_id_type=MESH)
            return carry

        lax.fori_loop(1, size, one, 0)

    greet("chan", me_c, NC)
    greet("space", me_s, NS)

    def cell_block(p, t):
        return (
            pl.ds(pl.multiple_of(t * HH + p // 4 * 8, 8), 8),
            pl.ds(pl.multiple_of(lax.rem(p, 4) * 128, 128), 128),
        )

    flight = {}

    def arrive(ref, channel):
        pltpu.make_async_copy(ref, ref, recv_sem.at[channel]).wait()

    def leave(channel):
        ref = flight.pop(channel)
        pltpu.make_async_copy(ref, ref, send_sem.at[channel]).wait()

    def send_all(channel, axis, pair):
        me, size = (me_c, NC) if axis == "chan" else (me_s, NS)

        def one(i, carry):
            if axis == "chan":
                p = lax.rem(me // 2 + i // 2 + 2, 4) * 2 + lax.rem(me + i, 2)
            else:
                p = lax.rem(me // 4 + i // 4 + 2, 4) * 4 + lax.rem(me + i + 2, 4)
            src, dst = pair(p)
            pltpu.make_async_remote_copy(
                src_ref=src,
                dst_ref=dst,
                send_sem=send_sem.at[channel],
                recv_sem=recv_sem.at[channel],
                device_id={axis: p},
                device_id_type=MESH,
            ).start()
            return carry

        own = 4 if axis == "chan" else 10
        lax.fori_loop(0, own, one, 0)
        lax.fori_loop(own + 1, size, one, 0)

    for t in range(2):
        loads[t].wait()

        for p in range(NC):
            r, c = HH * t + 8 * (p // 4), 128 * (p % 4)
            x = f[:, r : r + 8, c : c + 128]
            total = jnp.sum(x, axis=0)
            d = x - total * (1.0 / CL)
            part[p, t, 0] = total
            part[p, t, 1] = jnp.sum(d * d, axis=0)
    pl.semaphore_wait(barrier, NC + NS - 2)
    send_all(0, "chan", lambda p: (part.at[p], parts.at[me_c]))
    flight[0] = part.at[pl.ds(0, NC - 1)]
    parts[me_c] = part[me_c]
    for load in loads[2:]:
        load.start()

    for load in loads[2:6]:
        load.wait()
    lift = jnp.concatenate(
        [
            iota((4 * BS, BS), 0) // 2 % BS == iota((4 * BS, BS), 1),
            iota((4 * BS, BS), 0) % BS == iota((4 * BS, BS), 1),
        ],
        axis=0,
    ).astype(F32)
    weights = jnp.concatenate([spec_one[...].reshape(4 * BS, BS), spec_two[...].reshape(4 * BS, BS)], axis=0)
    lifted = exact_dot(lift, weights, NT)
    high = lifted.astype(BF16)
    rest = lifted - high.astype(F32)
    middle_term = rest.astype(BF16)
    low = (rest - middle_term.astype(F32)).astype(BF16)
    wide = (iota((8 * BS, 8 * ROWS), 1) // (2 * KC) == iota((8 * BS, 8 * ROWS), 0)).astype(BF16)
    lane = iota((8 * BS, 8 * 128), 1)
    slim = ((lane // 128 * BS + lane % BS == iota((8 * BS, 8 * 128), 0)) & (lane % 128 < 2 * BS)).astype(BF16)

    def spread(rows, table):
        terms = jnp.concatenate([high[rows], middle_term[rows], low[rows]], axis=0)
        terms = dot(terms, table)
        return terms[: 4 * BS] + (terms[4 * BS : 8 * BS] + terms[8 * BS :])

    def complex_form(values, width, part_out, part_in, layer, b):
        variant = iota((4 * BS, width), 0) // (2 * BS)
        real = values[:, (4 * layer + b) * width : (4 * layer + b + 1) * width]
        imag = values[:, (4 * layer + 2 + b) * width : (4 * layer + 2 + b + 1) * width]
        real = jnp.where((variant == 1) & (part_out == 1), -real, real)
        imag = jnp.where((variant == 0) & (part_out == 0), -imag, imag)
        return jnp.where(part_out == part_in, real, imag)

    big = spread(slice(0, 4 * BS), wide)
    small = spread(slice(4 * BS, 8 * BS), slim)
    same_column = iota((KC, ROWS), 1) % KC == iota((KC, ROWS), 0)
    for b in range(NBL):
        for layer in range(2):
            part_out, part_in = iota((4 * BS, ROWS), 0) % 2, iota((4 * BS, ROWS), 1) // KC % 2
            rw[2 * b + layer] = complex_form(big, ROWS, part_out, part_in, layer, b)
            for r in range(4 * BS if layer == 0 else 2 * BS):
                row_high, row_low = split(jnp.where(same_column, rw[2 * b + layer, r : r + 1, :], 0.0))
                to_high, to_low = ((m1h, m1l), (m2h, m2l))[layer]
                to_high[b, KC * r : KC * r + KC] = row_high
                to_low[b, KC * r : KC * r + KC] = row_low
            part_out, part_in = iota((4 * BS, 128), 0) // BS % 2, iota((4 * BS, 128), 1) // BS % 2
            form = complex_form(small, 128, part_out, part_in, layer, b)
            if layer == 0:
                x1h[b], x1l[b] = split(form)
            else:
                x2h[b], x2l[b] = split(form[: 2 * BS])

    arrive(parts.at[pl.ds(0, NC - 1)], 0)
    totals = parts[:, :, 0]
    mean = jnp.sum(totals, axis=0) * (1.0 / C)
    apart = totals * (1.0 / CL) - mean
    var = (jnp.sum(parts[:, :, 1], axis=0) + CL * jnp.sum(apart * apart, axis=0)) * (1.0 / C)
    moments[me_c, :, 0] = mean
    moments[me_c, :, 1] = lax.rsqrt(var + 1e-05)
    send_all(2, "chan", lambda p: (moments.at[me_c], moments.at[me_c]))
    flight[2] = moments.at[pl.ds(0, NC - 1)]

    load_in.wait()
    load_out.wait()
    w1h[...], w1l[...] = split(w1f[...] * gain_two[...])
    w2h[...], w2l[...] = split(w2f[...])
    load_width.wait()

    arrive(moments.at[pl.ds(0, NC - 1)], 2)
    for b in range(NBL):
        for t in range(2):
            for i in range(2):
                both = []
                for k in (i, i + 2):
                    both.append([jnp.concatenate([moments[k, t, m], moments[k + 4, t, m]], axis=0) for m in range(2)])
                for ch in range(BS):
                    x, x_two = (
                        (f[BS * b + ch, HH * t : HH * t + HH, c : c + 128] - mean) * scale * gain_one[BS * b + ch]
                        for c, (mean, scale) in zip((128 * i, HALF + 128 * i), both)
                    )
                    row = (BS * t + ch) * HH
                    rows, lanes = slice(row, row + HH), slice(128 * i, 128 * i + 128)
                    nh[0, rows, lanes], nl[0, rows, lanes] = split(x + x_two)
                    nh[1, rows, lanes], nl[1, rows, lanes] = split(x - x_two)

        for j in range(2):
            y = dot3((wd[0, j], wd[1, j]), (nh[j], nl[j]), NT)
            for t in range(2):
                fwd[b, 8 * j : 8 * j + 8, t] = y[:, 128 * t : 128 * t + 128].reshape(8, 2 * KC, 128)

        if b == 1:
            leave(4)
        send_all(4 + b, "space", lambda p: (fwd.at[b, p], got.at[b, me_s]))
        flight[4 + b] = fwd.at[b, pl.ds(0, NS - 1)]
        got[b, me_s] = fwd[b, me_s]
    load_there.wait()
    load_here.wait()

    special = (iota((KC, H), 0) == 0) & (me_s == 0)
    keep = jnp.where(special, 0.0, 1.0)

    def send_rows(b, t):
        channel = 8 + 2 * b + t
        send_all(channel, "space", lambda p: (inv.at[b, t, p], back.at[b, t, me_s]))
        flight[channel] = inv.at[b, t, pl.ds(0, NS - 1)]
        back[b, t, me_s] = inv[b, t, me_s]

    def spectral(b, between=None):
        arrive(got.at[b, pl.ds(0, NS - 1)], 4 + b)
        for t in range(2):
            near = swap_eighths([got[b, a, t] for a in range(8)])
            far = swap_eighths([got[b, 8 + a, t] for a in range(8)])
            for ch in range(BS):
                rows, lanes = slice(2 * KC * ch, 2 * KC * ch + 2 * KC), slice(128 * t, 128 * t + 128)
                xh[0, rows, lanes], xl[0, rows, lanes] = split(near[ch] + far[ch])
                xh[1, rows, lanes], xl[1, rows, lanes] = split(near[ch] - far[ch])

        both = []
        for n in range(2):
            x = dot3((xh[n], xl[n]), (ht[0, n], ht[1, n]))
            both.append((x[:, :HALF], x[:, HALF:]))
        xc, xs = (jnp.concatenate(pair, axis=1).reshape(BS, 2, KC, H) for pair in zip(*both))
        y = jnp.stack([xc[:, 0] + keep * xs[:, 1], keep * xc[:, 1] - xs[:, 0]], axis=1).reshape(ROWS, H)
        first = jnp.maximum(dot3((m1h[b], m1l[b]), split(y)), 0.0)
        m2 = m2h[b], m2l[b]
        one = shrink(dot3(m2, split(first[:ROWS]))).reshape(BS, 2, KC, H)
        two = shrink(dot3(m2, split(first[ROWS:]))).reshape(BS, 2, KC, H)
        real = one[:, 0] + two[:, 0]
        imag = one[:, 1] - two[:, 1]
        channel = iota((BS, H), 0)
        extra_real, extra_imag = jnp.zeros((BS, H), F32), jnp.zeros((BS, H), F32)
        for ch in range(BS):
            extra_real = jnp.where(channel == ch, xc[ch, 1, 0:1], extra_real)
            extra_imag = jnp.where(channel == ch, -xs[ch, 1, 0:1], extra_imag)
        extra = jnp.concatenate([extra_real, extra_imag], axis=0)
        first = jnp.maximum(dot3((x1h[b, :, : 2 * BS], x1l[b, :, : 2 * BS]), split(extra)), 0.0)
        x2 = x2h[b, :, : 2 * BS], x2l[b, :, : 2 * BS]
        one = shrink(dot3(x2, split(first[: 2 * BS])))
        two = shrink(dot3(x2, split(first[2 * BS :])))
        extra_real = one[:BS] + two[:BS]
        extra_imag = one[BS:] - two[BS:]
        for ch in range(BS):
            z_real = jnp.where(special, 0.5 * (real[ch] - extra_imag[ch : ch + 1]), real[ch])
            z_imag = jnp.where(special, 0.5 * (imag[ch] + extra_real[ch : ch + 1]), imag[ch])
            for i, z in enumerate((z_real, z_imag)):
                rows = slice((2 * ch + i) * KC, (2 * ch + i + 1) * KC)
                for n in range(2):
                    zh[n, rows], zl[n, rows] = split(z[:, HALF * n : HALF * n + HALF])

        for t in range(2):
            sums = []
            for n in range(2):
                z = dot3((zh[n], zl[n]), (hb[0, n, t], hb[1, n, t]))
                zc = z[:, :128].reshape(BS, 2, KC, 128)
                zs = z[:, 128:].reshape(BS, 2, KC, 128)
                sums.append(jnp.stack([zc[:, 0] - zs[:, 1], zc[:, 1] + zs[:, 0]], axis=1).reshape(BS, 2 * KC, 128))
            near = swap_eighths([sums[0][ch] + sums[1][ch] for ch in range(BS)])
            far = swap_eighths([sums[0][ch] - sums[1][ch] for ch in range(BS)])
            for a in range(8):
                inv[b, t, a] = near[a]
                inv[b, t, 8 + a] = far[a]
            if t == 0:
                send_rows(b, t)
                if between is not None:
                    between()

    def residual(b, t):
        channels = slice(BS * b, BS * b + BS)
        arrive(back.at[b, t, pl.ds(0, NS - 1)], 8 + 2 * b + t)
        sums = []
        for j in range(2):
            columns = split(back[b, t, 8 * j : 8 * j + 8].reshape(HALF, 128).T)
            sums.append(dot3(columns, (wd[0, j], wd[1, j])))
        rows = slice(HH * t, HH * t + HH)
        mixed[channels, rows, :HALF] = f[channels, rows, :HALF] + (sums[0] + sums[1]).reshape(BS, HH, HALF)
        mixed[channels, rows, HALF:] = f[channels, rows, HALF:] + (sums[0] - sums[1]).reshape(BS, HH, HALF)

        def pair(p):
            rows, lanes = cell_block(p, t)
            return mixed.at[pl.ds(BS * b, BS), rows, lanes], cells.at[t, me_c, pl.ds(BS * b, BS)]

        channel = 12 + 2 * b + t
        send_all(channel, "chan", pair)
        flight[channel] = cells.at[t, pl.ds(0, NC - 1), pl.ds(BS * b, BS)]
        rows, lanes = cell_block(me_c, t)
        cells[t, me_c, channels] = mixed[channels, rows, lanes]

    own = []

    def channel_mlp(t):
        for b in range(NBL):
            arrive(cells.at[t, pl.ds(0, NC - 1), pl.ds(BS * b, BS)], 12 + 2 * b + t)
        x = cells[t].reshape(C, 8, 128)
        mean = jnp.sum(x, axis=0) * (1.0 / C)
        d = x - mean
        scale = lax.rsqrt(jnp.sum(d * d, axis=0) * (1.0 / C) + 1e-05)
        n2[...] = (d * scale).reshape(C * 8, 128)
        x = jnp.concatenate([n2[pl.ds(i, C, stride=8), :] for i in range(8)], axis=1)
        v = gelu(dot3((w1h[...], w1l[...]), split(x)))
        y = dot3((w2h[...], w2l[...]), split(v))
        for i in range(8):
            ob[pl.ds(i, C, stride=8), :] = y[:, 128 * i : 128 * i + 128]
        ps[t] = cells[t] + ob[...].reshape(NC, CL, 8, 128)

        rows, lanes = cell_block(me_c, t)
        place = out.at[:, rows, lanes]
        send_all(16 + t, "chan", lambda p: (ps.at[t, p], place))
        flight[16 + t] = ps.at[t, pl.ds(0, NC - 1)]
        own.append(pltpu.make_async_copy(ps.at[t, me_c], place, load_sem.at[11 + t]))
        own[t].start()

    spectral(0)
    send_rows(0, 1)
    spectral(1, lambda: residual(0, 0))
    residual(0, 1)
    leave(10)
    send_rows(1, 1)
    residual(1, 0)
    residual(1, 1)
    for t in range(2):
        channel_mlp(t)
    for channel in sorted(flight):
        leave(channel)
    for t in range(2):
        own[t].wait()
        arrive(ps.at[t, pl.ds(0, NC - 1)], 16 + t)


def local(field, gain_one, spec_one, spec_two, gain_two, mlp_in, mlp_out):
    hbm = pl.BlockSpec(memory_space=pl.ANY)
    tables = [jnp.asarray(table) for table in (width_table(), *height_table())]
    scratch = [
        ((2, NBL, BS, BS), F32),
        ((2, NBL, BS, BS), F32),
        ((1, C), F32),
        ((CL, HL, H), F32),
        ((2, 2, HALF, HALF), BF16),
        ((2, 2, HALF, H), BF16),
        ((2, 2, 2, HALF, HALF), BF16),
        ((HID, C), F32),
        ((C, HID), F32),
        ((HID, C), BF16),
        ((HID, C), BF16),
        ((C, HID), BF16),
        ((C, HID), BF16),
        ((2 * NBL, 4 * BS, ROWS), F32),
        ((NBL, 2 * ROWS, ROWS), BF16),
        ((NBL, 2 * ROWS, ROWS), BF16),
        ((NBL, ROWS, ROWS), BF16),
        ((NBL, ROWS, ROWS), BF16),
        ((NBL, 4 * BS, 128), BF16),
        ((NBL, 4 * BS, 128), BF16),
        ((NBL, 2 * BS, 128), BF16),
        ((NBL, 2 * BS, 128), BF16),
        ((NC, 2, 2, 8, 128), F32),
        ((NC, 2, 2, 8, 128), F32),
        ((NC, 2, 2, 8, 128), F32),
        ((2, CL * HH, HALF), BF16),
        ((2, CL * HH, HALF), BF16),
        ((NBL, NS, 2, 2 * KC, 128), F32),
        ((NBL, NS, 2, 2 * KC, 128), F32),
        ((2, ROWS, HALF), BF16),
        ((2, ROWS, HALF), BF16),
        ((2, ROWS, HALF), BF16),
        ((2, ROWS, HALF), BF16),
        ((2, 2, NS, 2 * KC, 128), F32),
        ((2, 2, NS, 2 * KC, 128), F32),
        ((CL, HL, H), F32),
        ((2, NC, CL, 8, 128), F32),
        ((C * 8, 128), F32),
        ((C * 8, 128), F32),
        ((2, NC, CL, 8, 128), F32),
    ]
    return pl.pallas_call(
        kernel,
        out_shape=pltpu.VMEM((CL, HL, H), F32),
        in_specs=[hbm] * 10,
        out_specs=pl.BlockSpec(memory_space=pltpu.VMEM),
        scratch_shapes=[pltpu.SMEM((CL,), F32)]
        + [pltpu.VMEM(shape, dtype) for shape, dtype in scratch]
        + [pltpu.SemaphoreType.DMA((13,)), pltpu.SemaphoreType.DMA((18,)), pltpu.SemaphoreType.DMA((18,))],
        compiler_params=pltpu.CompilerParams(
            collective_id=0, has_side_effects=True, vmem_limit_bytes=56 * 1024 * 1024
        ),
        name="afno_block",
    )(gain_one, spec_one, spec_two, gain_two.reshape(1, C), field, mlp_in, mlp_out, *tables)


def solution(mesh):
    placed = (
        P("chan", "space", None),
        P("chan"),
        P(None, "chan", None, None),
        P(None, "chan", None, None),
        P(),
        P(),
        P(),
    )
    return jax.shard_map(
        local, mesh=mesh, in_specs=placed, out_specs=P("chan", "space", None), check_vma=False
    )
```

```python
import functools

import jax
import jax.numpy as jnp
import ml_dtypes
import numpy as np
from jax import lax
from jax.experimental import pallas as pl
from jax.experimental.pallas import tpu as pltpu
from jax.sharding import PartitionSpec as P

MESH = pl.DeviceIdType.MESH
F32 = jnp.float32
BF16 = jnp.bfloat16

H = 512
C = 128
HID = 512
NS = 16
NC = 8
CL = C // NC
HL = H // NS
BS = 8
NBL = CL // BS
KC = 16
ROWS = BS * 2 * KC
HALF = H // 2
HH = HL // 2

NN = ((1,), (0,))
NT = ((1,), (1,))


def halves(table):
    high = table.astype(ml_dtypes.bfloat16)
    low = (table - high.astype(np.float64)).astype(ml_dtypes.bfloat16)
    return np.stack([high, low])


def width_table():
    row = np.arange(HALF)
    number = (row // (2 * KC)) * KC + row % KC
    imag = (row // KC) % 2 == 1
    both = []
    for odd in (0, 1):
        nyquist = imag & (number == 0) & (odd == 0)
        freq = np.where(nyquist, H // 2, 2 * number + odd)
        angle = 2 * np.pi / H * (freq[:, None] * np.arange(HALF)[None, :] % H)
        both.append(np.where((imag & ~nyquist)[:, None], -np.sin(angle), np.cos(angle)) / np.sqrt(H))
    return halves(np.stack(both))


def height_table():
    index = np.arange(HALF)
    h = index % 128 // HH * HL + index // 128 * HH + index % HH
    there, back = [], []
    for odd in (0, 1):
        angle = 2 * np.pi / H * (h[:, None] * (2 * index + odd)[None, :] % H)
        cosine, sine = np.cos(angle) / np.sqrt(H), np.sin(angle) / np.sqrt(H)
        there.append(np.concatenate([cosine, sine], axis=1))
        back.append(np.stack([np.concatenate([cosine.T[:, k], sine.T[:, k]], axis=1) for k in np.split(index, 2)]))
    return halves(np.stack(there)), halves(np.stack(back))


def split(x):
    high = x.astype(BF16)
    return high, (x - high.astype(F32)).astype(BF16)


def dot(a, b, dims=NN):
    return lax.dot_general(a, b, (dims, ((), ())), preferred_element_type=F32)


def dot3(a, b, dims=NN):
    left = jnp.concatenate([a[0], a[0], a[1]], axis=dims[0][0])
    right = jnp.concatenate([b[0], b[1], b[0]], axis=dims[1][0])
    return dot(left, right, dims)


def exact_dot(a, b, dims=NN):
    return lax.dot_general(a, b, (dims, ((), ())), precision=lax.Precision.HIGHEST, preferred_element_type=F32)


def iota(shape, axis):
    return lax.broadcasted_iota(jnp.int32, shape, axis)


def gelu(v):
    return 0.5 * v * (1.0 + lax.erf(v * 2.0**-0.5))


def shrink(v):
    return jnp.maximum(v - 0.01, 0.0) + jnp.minimum(v + 0.01, 0.0)


def swap_eighths(tiles):
    tiles = list(tiles)
    lane = iota(tiles[0].shape, 1)
    for step in (4, 2, 1):
        width = 16 * step
        low = lane // width % 2 == 0
        for i in range(8):
            if i & step == 0:
                one, two = tiles[i], tiles[i + step]
                tiles[i] = jnp.where(low, one, pltpu.roll(two, width, 1))
                tiles[i + step] = jnp.where(low, pltpu.roll(one, 128 - width, 1), two)
    return tiles


def kernel(
    gain_one_in, spec_one_in, spec_two_in, gain_two_in, field, mlp_in, mlp_out, width, there, here, out,
    gain_one, spec_one, spec_two, gain_two, f, wd, ht, hb, w1f, w2f, w1h, w1l, w2h, w2l, rw, m1h, m1l, m2h, m2l, x1h, x1l, x2h, x2l,
    part, parts, moments, nh, nl, fwd, got, xh, xl, zh, zl, inv, back, mixed, cells, n2, ob, ps,
    load_sem, send_sem, recv_sem,
):
    me_s = lax.axis_index("space")
    me_c = lax.axis_index("chan")

    loads = [(field.at[:, pl.ds(16 * i, 16)], f.at[:, pl.ds(16 * i, 16)]) for i in range(2)]
    loads += [(spec_one_in, spec_one), (spec_two_in, spec_two), (gain_one_in, gain_one), (gain_two_in, gain_two)]
    loads += [(width, wd), (there, ht), (here, hb), (mlp_in, w1f), (mlp_out, w2f)]
    loads = [pltpu.make_async_copy(src, dst, load_sem.at[i]) for i, (src, dst) in enumerate(loads)]
    for load in loads[:2]:
        load.start()
    load_width, load_there, load_here, load_in, load_out = loads[6:]

    barrier = pltpu.get_barrier_semaphore()

    def greet(axis, me, size):
        def one(i, carry):
            pl.semaphore_signal(barrier, inc=1, device_id={axis: lax.rem(me + i, size)}, device_id_type=MESH)
            return carry

        lax.fori_loop(1, size, one, 0)

    greet("chan", me_c, NC)
    greet("space", me_s, NS)

    def cell_block(p, t):
        return (
            pl.ds(pl.multiple_of(t * HH + p // 4 * 8, 8), 8),
            pl.ds(pl.multiple_of(lax.rem(p, 4) * 128, 128), 128),
        )

    flight = {}

    def far(k):
        g = lax.rem(k + 2, 4)
        return g + k // 2 * (1 - 2 * g)

    def arrive(ref, channel):
        pltpu.make_async_copy(ref, ref, recv_sem.at[channel]).wait()

    def leave(channel):
        ref = flight.pop(channel)
        pltpu.make_async_copy(ref, ref, send_sem.at[channel]).wait()

    def send_all(channel, axis, pair):
        me, size = (me_c, NC) if axis == "chan" else (me_s, NS)

        def one(i, carry):
            k = i // 2 if axis == "chan" else i // 4
            step = far(k)
            if axis == "chan":
                p = lax.rem(me // 2 + step, 4) * 2 + lax.rem(me + i + 1, 2)
            else:
                p = lax.rem(me // 4 + step, 4) * 4 + lax.rem(lax.rem(me, 4) + far(lax.rem(i, 4)), 4)
            src, dst = pair(p)
            pltpu.make_async_remote_copy(
                src_ref=src,
                dst_ref=dst,
                send_sem=send_sem.at[channel],
                recv_sem=recv_sem.at[channel],
                device_id={axis: p},
                device_id_type=MESH,
            ).start()
            return carry

        lax.fori_loop(0, size - 1, one, 0)

    for t in range(2):
        loads[t].wait()

        for p in range(NC):
            r, c = HH * t + 8 * (p // 4), 128 * (p % 4)
            x = f[:, r : r + 8, c : c + 128]
            total = jnp.sum(x, axis=0)
            d = x - total * (1.0 / CL)
            part[p, t, 0] = total
            part[p, t, 1] = jnp.sum(d * d, axis=0)
    pl.semaphore_wait(barrier, NC + NS - 2)
    send_all(0, "chan", lambda p: (part.at[p], parts.at[me_c]))
    flight[0] = part.at[pl.ds(0, NC - 1)]
    parts[me_c] = part[me_c]
    for load in loads[2:]:
        load.start()

    for load in loads[2:6]:
        load.wait()
    lift = jnp.concatenate(
        [
            iota((4 * BS, BS), 0) // 2 % BS == iota((4 * BS, BS), 1),
            iota((4 * BS, BS), 0) % BS == iota((4 * BS, BS), 1),
        ],
        axis=0,
    ).astype(F32)
    weights = jnp.concatenate([spec_one[...].reshape(4 * BS, BS), spec_two[...].reshape(4 * BS, BS)], axis=0)
    lifted = exact_dot(lift, weights, NT)
    high = lifted.astype(BF16)
    rest = lifted - high.astype(F32)
    middle_term = rest.astype(BF16)
    low = (rest - middle_term.astype(F32)).astype(BF16)
    wide = (iota((8 * BS, 8 * ROWS), 1) // (2 * KC) == iota((8 * BS, 8 * ROWS), 0)).astype(BF16)
    lane = iota((8 * BS, 8 * 128), 1)
    slim = ((lane // 128 * BS + lane % BS == iota((8 * BS, 8 * 128), 0)) & (lane % 128 < 2 * BS)).astype(BF16)

    def spread(rows, table):
        terms = jnp.concatenate([high[rows], middle_term[rows], low[rows]], axis=0)
        terms = dot(terms, table)
        return terms[: 4 * BS] + (terms[4 * BS : 8 * BS] + terms[8 * BS :])

    def complex_form(values, width, part_out, part_in, layer, b):
        variant = iota((4 * BS, width), 0) // (2 * BS)
        real = values[:, (4 * layer + b) * width : (4 * layer + b + 1) * width]
        imag = values[:, (4 * layer + 2 + b) * width : (4 * layer + 2 + b + 1) * width]
        real = jnp.where((variant == 1) & (part_out == 1), -real, real)
        imag = jnp.where((variant == 0) & (part_out == 0), -imag, imag)
        return jnp.where(part_out == part_in, real, imag)

    big = spread(slice(0, 4 * BS), wide)
    small = spread(slice(4 * BS, 8 * BS), slim)
    same_column = iota((KC, ROWS), 1) % KC == iota((KC, ROWS), 0)
    for b in range(NBL):
        for layer in range(2):
            part_out, part_in = iota((4 * BS, ROWS), 0) % 2, iota((4 * BS, ROWS), 1) // KC % 2
            rw[2 * b + layer] = complex_form(big, ROWS, part_out, part_in, layer, b)
            for r in range(4 * BS if layer == 0 else 2 * BS):
                row_high, row_low = split(jnp.where(same_column, rw[2 * b + layer, r : r + 1, :], 0.0))
                to_high, to_low = ((m1h, m1l), (m2h, m2l))[layer]
                to_high[b, KC * r : KC * r + KC] = row_high
                to_low[b, KC * r : KC * r + KC] = row_low
            part_out, part_in = iota((4 * BS, 128), 0) // BS % 2, iota((4 * BS, 128), 1) // BS % 2
            form = complex_form(small, 128, part_out, part_in, layer, b)
            if layer == 0:
                x1h[b], x1l[b] = split(form)
            else:
                x2h[b], x2l[b] = split(form[: 2 * BS])

    arrive(parts.at[pl.ds(0, NC - 1)], 0)
    totals = parts[:, :, 0]
    mean = jnp.sum(totals, axis=0) * (1.0 / C)
    apart = totals * (1.0 / CL) - mean
    var = (jnp.sum(parts[:, :, 1], axis=0) + CL * jnp.sum(apart * apart, axis=0)) * (1.0 / C)
    moments[me_c, :, 0] = mean
    moments[me_c, :, 1] = lax.rsqrt(var + 1e-05)
    send_all(2, "chan", lambda p: (moments.at[me_c], moments.at[me_c]))
    flight[2] = moments.at[pl.ds(0, NC - 1)]

    load_in.wait()
    load_out.wait()
    w1h[...], w1l[...] = split(w1f[...] * gain_two[...])
    w2h[...], w2l[...] = split(w2f[...])
    load_width.wait()

    arrive(moments.at[pl.ds(0, NC - 1)], 2)
    for b in range(NBL):
        for t in range(2):
            for i in range(2):
                both = []
                for k in (i, i + 2):
                    both.append([jnp.concatenate([moments[k, t, m], moments[k + 4, t, m]], axis=0) for m in range(2)])
                for ch in range(BS):
                    x, x_two = (
                        (f[BS * b + ch, HH * t : HH * t + HH, c : c + 128] - mean) * scale * gain_one[BS * b + ch]
                        for c, (mean, scale) in zip((128 * i, HALF + 128 * i), both)
                    )
                    row = (BS * t + ch) * HH
                    rows, lanes = slice(row, row + HH), slice(128 * i, 128 * i + 128)
                    nh[0, rows, lanes], nl[0, rows, lanes] = split(x + x_two)
                    nh[1, rows, lanes], nl[1, rows, lanes] = split(x - x_two)

        for j in range(2):
            y = dot3((wd[0, j], wd[1, j]), (nh[j], nl[j]), NT)
            for t in range(2):
                fwd[b, 8 * j : 8 * j + 8, t] = y[:, 128 * t : 128 * t + 128].reshape(8, 2 * KC, 128)

        if b == 1:
            leave(4)
        send_all(4 + b, "space", lambda p: (fwd.at[b, p], got.at[b, me_s]))
        flight[4 + b] = fwd.at[b, pl.ds(0, NS - 1)]
        got[b, me_s] = fwd[b, me_s]
    load_there.wait()
    load_here.wait()

    special = (iota((KC, H), 0) == 0) & (me_s == 0)
    keep = jnp.where(special, 0.0, 1.0)

    def send_rows(b, t):
        channel = 8 + 2 * b + t
        send_all(channel, "space", lambda p: (inv.at[b, t, p], back.at[b, t, me_s]))
        flight[channel] = inv.at[b, t, pl.ds(0, NS - 1)]
        back[b, t, me_s] = inv[b, t, me_s]

    def spectral(b, between=None):
        arrive(got.at[b, pl.ds(0, NS - 1)], 4 + b)
        for t in range(2):
            near = swap_eighths([got[b, a, t] for a in range(8)])
            far = swap_eighths([got[b, 8 + a, t] for a in range(8)])
            for ch in range(BS):
                rows, lanes = slice(2 * KC * ch, 2 * KC * ch + 2 * KC), slice(128 * t, 128 * t + 128)
                xh[0, rows, lanes], xl[0, rows, lanes] = split(near[ch] + far[ch])
                xh[1, rows, lanes], xl[1, rows, lanes] = split(near[ch] - far[ch])

        both = []
        for n in range(2):
            x = dot3((xh[n], xl[n]), (ht[0, n], ht[1, n]))
            both.append((x[:, :HALF], x[:, HALF:]))
        xc, xs = (jnp.concatenate(pair, axis=1).reshape(BS, 2, KC, H) for pair in zip(*both))
        y = jnp.stack([xc[:, 0] + keep * xs[:, 1], keep * xc[:, 1] - xs[:, 0]], axis=1).reshape(ROWS, H)
        first = jnp.maximum(dot3((m1h[b], m1l[b]), split(y)), 0.0)
        m2 = m2h[b], m2l[b]
        one = shrink(dot3(m2, split(first[:ROWS]))).reshape(BS, 2, KC, H)
        two = shrink(dot3(m2, split(first[ROWS:]))).reshape(BS, 2, KC, H)
        real = one[:, 0] + two[:, 0]
        imag = one[:, 1] - two[:, 1]
        channel = iota((BS, H), 0)
        extra_real, extra_imag = jnp.zeros((BS, H), F32), jnp.zeros((BS, H), F32)
        for ch in range(BS):
            extra_real = jnp.where(channel == ch, xc[ch, 1, 0:1], extra_real)
            extra_imag = jnp.where(channel == ch, -xs[ch, 1, 0:1], extra_imag)
        extra = jnp.concatenate([extra_real, extra_imag], axis=0)
        first = jnp.maximum(dot3((x1h[b, :, : 2 * BS], x1l[b, :, : 2 * BS]), split(extra)), 0.0)
        x2 = x2h[b, :, : 2 * BS], x2l[b, :, : 2 * BS]
        one = shrink(dot3(x2, split(first[: 2 * BS])))
        two = shrink(dot3(x2, split(first[2 * BS :])))
        extra_real = one[:BS] + two[:BS]
        extra_imag = one[BS:] - two[BS:]
        for ch in range(BS):
            z_real = jnp.where(special, 0.5 * (real[ch] - extra_imag[ch : ch + 1]), real[ch])
            z_imag = jnp.where(special, 0.5 * (imag[ch] + extra_real[ch : ch + 1]), imag[ch])
            for i, z in enumerate((z_real, z_imag)):
                rows = slice((2 * ch + i) * KC, (2 * ch + i + 1) * KC)
                for n in range(2):
                    zh[n, rows], zl[n, rows] = split(z[:, HALF * n : HALF * n + HALF])

        for t in range(2):
            sums = []
            for n in range(2):
                z = dot3((zh[n], zl[n]), (hb[0, n, t], hb[1, n, t]))
                zc = z[:, :128].reshape(BS, 2, KC, 128)
                zs = z[:, 128:].reshape(BS, 2, KC, 128)
                sums.append(jnp.stack([zc[:, 0] - zs[:, 1], zc[:, 1] + zs[:, 0]], axis=1).reshape(BS, 2 * KC, 128))
            near = swap_eighths([sums[0][ch] + sums[1][ch] for ch in range(BS)])
            far = swap_eighths([sums[0][ch] - sums[1][ch] for ch in range(BS)])
            for a in range(8):
                inv[b, t, a] = near[a]
                inv[b, t, 8 + a] = far[a]
            if t == 0:
                send_rows(b, t)
                if between is not None:
                    between()

    def residual(b, t):
        channels = slice(BS * b, BS * b + BS)
        arrive(back.at[b, t, pl.ds(0, NS - 1)], 8 + 2 * b + t)
        sums = []
        for j in range(2):
            columns = split(back[b, t, 8 * j : 8 * j + 8].reshape(HALF, 128).T)
            sums.append(dot3(columns, (wd[0, j], wd[1, j])))
        rows = slice(HH * t, HH * t + HH)
        mixed[channels, rows, :HALF] = f[channels, rows, :HALF] + (sums[0] + sums[1]).reshape(BS, HH, HALF)
        mixed[channels, rows, HALF:] = f[channels, rows, HALF:] + (sums[0] - sums[1]).reshape(BS, HH, HALF)

        def pair(p):
            rows, lanes = cell_block(p, t)
            return mixed.at[pl.ds(BS * b, BS), rows, lanes], cells.at[t, me_c, pl.ds(BS * b, BS)]

        channel = 12 + 2 * b + t
        send_all(channel, "chan", pair)
        flight[channel] = cells.at[t, pl.ds(0, NC - 1), pl.ds(BS * b, BS)]
        rows, lanes = cell_block(me_c, t)
        cells[t, me_c, channels] = mixed[channels, rows, lanes]

    own = []

    def channel_mlp(t):
        for b in range(NBL):
            arrive(cells.at[t, pl.ds(0, NC - 1), pl.ds(BS * b, BS)], 12 + 2 * b + t)
        x = cells[t].reshape(C, 8, 128)
        mean = jnp.sum(x, axis=0) * (1.0 / C)
        d = x - mean
        scale = lax.rsqrt(jnp.sum(d * d, axis=0) * (1.0 / C) + 1e-05)
        n2[...] = (d * scale).reshape(C * 8, 128)
        x = jnp.concatenate([n2[pl.ds(i, C, stride=8), :] for i in range(8)], axis=1)
        v = gelu(dot3((w1h[...], w1l[...]), split(x)))
        y = dot3((w2h[...], w2l[...]), split(v))
        for i in range(8):
            ob[pl.ds(i, C, stride=8), :] = y[:, 128 * i : 128 * i + 128]
        ps[t] = cells[t] + ob[...].reshape(NC, CL, 8, 128)

        rows, lanes = cell_block(me_c, t)
        place = out.at[:, rows, lanes]
        send_all(16 + t, "chan", lambda p: (ps.at[t, p], place))
        flight[16 + t] = ps.at[t, pl.ds(0, NC - 1)]
        own.append(pltpu.make_async_copy(ps.at[t, me_c], place, load_sem.at[11 + t]))
        own[t].start()

    spectral(0)
    send_rows(0, 1)
    spectral(1, lambda: residual(0, 0))
    residual(0, 1)
    leave(10)
    send_rows(1, 1)
    residual(1, 0)
    residual(1, 1)
    for t in range(2):
        channel_mlp(t)
    for channel in sorted(flight):
        leave(channel)
    for t in range(2):
        own[t].wait()
        arrive(ps.at[t, pl.ds(0, NC - 1)], 16 + t)


def local(field, gain_one, spec_one, spec_two, gain_two, mlp_in, mlp_out):
    hbm = pl.BlockSpec(memory_space=pl.ANY)
    tables = [jnp.asarray(table) for table in (width_table(), *height_table())]
    scratch = [
        ((2, NBL, BS, BS), F32),
        ((2, NBL, BS, BS), F32),
        ((1, C), F32),
        ((CL, HL, H), F32),
        ((2, 2, HALF, HALF), BF16),
        ((2, 2, HALF, H), BF16),
        ((2, 2, 2, HALF, HALF), BF16),
        ((HID, C), F32),
        ((C, HID), F32),
        ((HID, C), BF16),
        ((HID, C), BF16),
        ((C, HID), BF16),
        ((C, HID), BF16),
        ((2 * NBL, 4 * BS, ROWS), F32),
        ((NBL, 2 * ROWS, ROWS), BF16),
        ((NBL, 2 * ROWS, ROWS), BF16),
        ((NBL, ROWS, ROWS), BF16),
        ((NBL, ROWS, ROWS), BF16),
        ((NBL, 4 * BS, 128), BF16),
        ((NBL, 4 * BS, 128), BF16),
        ((NBL, 2 * BS, 128), BF16),
        ((NBL, 2 * BS, 128), BF16),
        ((NC, 2, 2, 8, 128), F32),
        ((NC, 2, 2, 8, 128), F32),
        ((NC, 2, 2, 8, 128), F32),
        ((2, CL * HH, HALF), BF16),
        ((2, CL * HH, HALF), BF16),
        ((NBL, NS, 2, 2 * KC, 128), F32),
        ((NBL, NS, 2, 2 * KC, 128), F32),
        ((2, ROWS, HALF), BF16),
        ((2, ROWS, HALF), BF16),
        ((2, ROWS, HALF), BF16),
        ((2, ROWS, HALF), BF16),
        ((2, 2, NS, 2 * KC, 128), F32),
        ((2, 2, NS, 2 * KC, 128), F32),
        ((CL, HL, H), F32),
        ((2, NC, CL, 8, 128), F32),
        ((C * 8, 128), F32),
        ((C * 8, 128), F32),
        ((2, NC, CL, 8, 128), F32),
    ]
    return pl.pallas_call(
        kernel,
        out_shape=pltpu.VMEM((CL, HL, H), F32),
        in_specs=[hbm] * 10,
        out_specs=pl.BlockSpec(memory_space=pltpu.VMEM),
        scratch_shapes=[pltpu.SMEM((CL,), F32)]
        + [pltpu.VMEM(shape, dtype) for shape, dtype in scratch]
        + [pltpu.SemaphoreType.DMA((13,)), pltpu.SemaphoreType.DMA((18,)), pltpu.SemaphoreType.DMA((18,))],
        compiler_params=pltpu.CompilerParams(
            collective_id=0, has_side_effects=True, vmem_limit_bytes=56 * 1024 * 1024
        ),
        name="afno_block",
    )(gain_one, spec_one, spec_two, gain_two.reshape(1, C), field, mlp_in, mlp_out, *tables)


def solution(mesh):
    placed = (
        P("chan", "space", None),
        P("chan"),
        P(None, "chan", None, None),
        P(None, "chan", None, None),
        P(),
        P(),
        P(),
    )
    return jax.shard_map(
        local, mesh=mesh, in_specs=placed, out_specs=P("chan", "space", None), check_vma=False
    )
```
